128 devices in a mesh: gx: 16 (over z, x_lo, core), gy: 8 (over y, x_hi).
Axes of the slice: x: 4 (x_hi: 2, x_lo: 2; x = x_hi * 2 + x_lo), y: 4, z: 4, core: 2. Of those that a mesh axis runs over, the one named last changes fastest.
Arguments:
- adj_disp: float32 [3, 128, 128, 128], P(None, 'gx', 'gy'), may hold values from -6 to 6
- adj_veloc: float32 [3, 128, 128, 128], P(None, 'gx', 'gy'), may hold values from -6 to 6
- fwd_disp: float32 [3, 128, 128, 128], P(None, 'gx', 'gy'), may hold values from -6 to 6
- inv_mass: float32 [128, 128, 128], P('gx', 'gy'), may hold values from 0.5 to 2
- shear_mod: float32 [32, 32, 32], P('gx', 'gy'), may hold values from 0.5 to 2
- lame_mod: float32 [32, 32, 32], P('gx', 'gy'), may hold values from 0.5 to 2
- kernel_mu: float32 [125, 32768], P(None, ('gx', 'gy')), may hold values from -6 to 6
- kernel_kappa: float32 [125, 32768], P(None, ('gx', 'gy')), may hold values from -6 to 6
- chan_window: float32 [16, 1048576], P(None, ('gx', 'gy')), may hold values from -24 to 24
- chan_dir: float32 [3, 1048576], P(None, ('gx', 'gy')), may hold values from -6 to 6
- chan_local: float32 [3, 1048576], P(None, ('gx', 'gy')), may hold values from -1 to 1
- chan_part: int32 [1048576, 1], P(('gx', 'gy')), may hold values from 0 to 127; in each aligned block of 8192 rows (0 to 8191, 8192 to 16383, ...) at most 128 rows name the same one
- chan_elem: int32 [1048576], P(('gx', 'gy')), may hold values from 0 to 255
Outputs:
- adj_disp_new: float32 [3, 128, 128, 128], P(None, 'gx', 'gy')
- adj_veloc_new: float32 [3, 128, 128, 128], P(None, 'gx', 'gy')
- kernel_mu_new: float32 [125, 32768], P(None, ('gx', 'gy'))
- kernel_kappa_new: float32 [125, 32768], P(None, ('gx', 'gy'))
The draws below stay inside these ranges and needn't reach their ends.
Inputs may be any that keep to these rules, and one draw needn't show every extreme that they name: `chan_part`: among the 8192 channels recorded by one partition, at most 128 lie in elements of any one owning partition, and in every draw some partition receives exactly 128 channels from some recording partition.
All inputs are finite; a program needn't handle non-finite values.
Results may differ from the reference program's by a relative error of at most 0.00005.
Values sent between devices are 32-bit elements; how exact they have to be, the bound alone decides.
No kernel may reach another device: no remote copies, remote signals or barrier semaphores. Data moves between devices by JAX's collectives and lax.ppermute only.
A program may use at most 128 MiB of HBM per device.

```python
import math
import jax
import jax.numpy as jnp
import numpy as np
from jax import lax

EX = 2
EY = 4
EZ = 32
CH_DEV = 8192
NGLL = 5
NSAMP = 16
NXG = 128
NYG = 128
NZ = 128
ELEM_DEV = 256
ELEM_TOTAL = 32768
CH_TOTAL = 1048576
CAP = 128
N_GX = 16
N_GY = 8
DEVICES = 128


def set_ends(drawn, rng, low, top_value):
    longest = drawn.shape.index(max(drawn.shape))
    spots = []
    for shift in (0, 1):
        where = [jax.random.randint(jax.random.fold_in(rng, axis), (), 0, length) for axis, length in enumerate(drawn.shape)]
        where[longest] = (where[longest] + shift) % drawn.shape[longest]
        spots.append(tuple(where))
    return drawn.at[spots[0]].set(low).at[spots[1]].set(top_value)


def steps_of(rng, extent, split, smallest, largest):
    loudness, own = 1.0, jax.random.fold_in(rng, 6)
    for position, parts in split:
        heights = jnp.exp(jax.random.uniform(jax.random.fold_in(own, position), (parts,), jnp.float32, smallest / len(split), largest / len(split)))
        loudness = loudness * jnp.repeat(heights, extent[position] // parts).reshape([-1 if axis == position else 1 for axis in range(len(extent))])
    return loudness


def routed_block(stream_key, own, number, rows, count, top, reach, skew):
    ranking = jax.random.permutation(stream_key, count)
    heavy_load, common = shares(count, rows * top, reach, skew, True), shares(count, rows * top, reach, skew, False)
    places = jnp.arange(count)

    def named(tallies, offset_by):
        used = int((tallies > 0).sum())
        fixed = max(1, used // 4)
        shifted = fixed + (places - fixed + offset_by * (used - fixed)) % max(1, count - fixed)
        return jnp.zeros((count,), jnp.int32).at[ranking[jnp.where(places < fixed, places, shifted)]].set(jnp.asarray(tallies, jnp.int32))

    tallies = jnp.where(number % 4 == 0, named(heavy_load, number // 4), named(common, number - number // 4 - 1))
    mixed = jax.random.permutation(jax.random.fold_in(own, 3), count)
    donor, taker = mixed[0:count // 2 * 2:2], mixed[1:count // 2 * 2:2]
    slack = jnp.minimum(tallies[donor] - 1, reach - tallies[taker]) // 2
    slack = jnp.where((donor == ranking[0]) | (taker == ranking[0]) | (tallies[taker] == 0), 0, jnp.maximum(slack, 0))
    shifted = jax.random.randint(jax.random.fold_in(own, 4), (count // 2,), 0, 1 << 20) % (slack + 1)
    tallies = tallies.at[donor].add(-shifted).at[taker].add(shifted)
    members = jnp.searchsorted(jnp.cumsum(tallies), jnp.arange(rows * top), side="right").astype(jnp.int32)
    grid = members.reshape(top, rows).T
    grid = grid[jax.random.permutation(jax.random.fold_in(own, 1), rows)]
    offset_by = jax.random.randint(jax.random.fold_in(own, 2), (rows, 1), 0, top)
    return jnp.take_along_axis(grid, (jnp.arange(top)[None, :] + offset_by) % top, axis=1)


def shares(amount, total, most, lean, full):
    portions = [(1 << 20) // math.isqrt(rank ** lean) + 1 for rank in range(1, amount + 1)]
    largest = most if full else min(most, max(-(-total // amount), total * portions[0] // sum(portions)))
    least = 1 if total - largest >= amount - 1 else 0
    holding, surplus = [largest] + [least] * (amount - 1), total - largest - least * (amount - 1)
    while surplus > 0:
        candidates = [i for i in range(1, amount) if holding[i] < largest] or [i for i in range(1, amount) if holding[i] < most]
        whole, left = sum([portions[i] for i in candidates]), surplus
        for i in candidates:
            more = min(most - holding[i], max(1, left * portions[i] // whole), surplus)
            holding[i] = holding[i] + more
            surplus = surplus - more
    return np.array(holding)


def noise(stream_key, shape, deviation, bound, shards=(), kind=jnp.bfloat16):
    result = jax.random.normal(stream_key, shape, jnp.float32) * deviation
    if len(shards) > 0:
        result = steps_of(stream_key, shape, shards, -0.22, 0.18) * result
    return jnp.clip(result, min=-bound, max=bound).astype(kind)


def setup_inputs(seed: int = 0) -> dict:
    seeds = jax.random.split(jax.random.key(seed), 14)
    adj_disp = noise(seeds[0], (3, NXG, NYG, NZ), 1.0, 6.0, ((1, 16), (2, 8)), jnp.float32)
    adj_veloc = noise(seeds[1], (3, NXG, NYG, NZ), 1.0, 6.0, ((1, 16), (2, 8)), jnp.float32)
    fwd_disp = noise(seeds[2], (3, NXG, NYG, NZ), 1.0, 6.0, ((1, 16), (2, 8)), jnp.float32)
    inv_mass = jnp.clip(jnp.exp(math.log(2.0) - 1.3862944 * jax.random.uniform(seeds[3], (NXG, NYG, NZ), jnp.float32) ** steps_of(seeds[3], (NXG, NYG, NZ), ((0, 16), (1, 8)), -0.2, 0.2)), 0.5, 2.0)
    shear_mod = jnp.clip(jnp.exp(math.log(2.0) - 1.3862944 * jax.random.uniform(seeds[4], (EX * N_GX, EY * N_GY, EZ), jnp.float32) ** steps_of(seeds[4], (EX * N_GX, EY * N_GY, EZ), ((0, 16), (1, 8)), -0.2, 0.2)), 0.5, 2.0)
    lame_mod = jnp.clip(jnp.exp(math.log(2.0) - 1.3862944 * jax.random.uniform(seeds[5], (EX * N_GX, EY * N_GY, EZ), jnp.float32) ** steps_of(seeds[5], (EX * N_GX, EY * N_GY, EZ), ((0, 16), (1, 8)), -0.2, 0.2)), 0.5, 2.0)
    kernel_mu = noise(seeds[6], (NGLL ** 3, ELEM_TOTAL), 1.0, 6.0, ((1, 128),), jnp.float32)
    kernel_kappa = noise(seeds[7], (NGLL ** 3, ELEM_TOTAL), 1.0, 6.0, ((1, 128),), jnp.float32)
    chan_window = noise(seeds[8], (NSAMP, CH_TOTAL), 4.0, 24.0, ((1, 128),), jnp.float32)
    chan_dir = noise(seeds[9], (3, CH_TOTAL), 1.0, 6.0, ((1, 128),), jnp.float32)
    chan_local = jnp.clip(jax.random.uniform(seeds[10], (3, CH_TOTAL), jnp.float32, -1.0, 1.0) * steps_of(seeds[10], (3, CH_TOTAL), ((1, 128),), -0.4, 0.0), -1.0, 1.0)
    chan_part_keys = jax.random.split(jax.random.fold_in(seeds[11], 1), CH_TOTAL // CH_DEV)
    chan_part_turns = jax.random.permutation(jax.random.fold_in(seeds[11], 3), CH_TOTAL // CH_DEV)
    chan_part = jax.vmap(lambda own, number: routed_block(jax.random.fold_in(seeds[11], 2), own, number, CH_DEV, DEVICES, 1, CAP, 2))(chan_part_keys, chan_part_turns).reshape((CH_TOTAL, 1))
    chan_elem = set_ends(jax.random.randint(seeds[12], (CH_TOTAL,), 0, ELEM_DEV), jax.random.fold_in(seeds[12], 1), 0, ELEM_DEV - 1).astype(jnp.int32)
    return {"adj_disp": adj_disp, "adj_veloc": adj_veloc, "fwd_disp": fwd_disp, "inv_mass": inv_mass, "shear_mod": shear_mod, "lame_mod": lame_mod, "kernel_mu": kernel_mu, "kernel_kappa": kernel_kappa, "chan_window": chan_window, "chan_dir": chan_dir, "chan_local": chan_local, "chan_part": chan_part, "chan_elem": chan_elem}


time_step = 0.05
highest = lax.Precision.HIGHEST

def gll_tables():
    gll_nodes = np.array([-1.0, -np.sqrt(3.0 / 7.0), 0.0, np.sqrt(3.0 / 7.0), 1.0])
    gll_weights = np.array([0.1, 49.0 / 90.0, 32.0 / 45.0, 49.0 / 90.0, 0.1])
    derivative = np.zeros((5, 5))
    for a in range(5):
        for p in range(5):
            summed = 0.0
            for m in range(5):
                if m != p:
                    factor = 1.0 / (gll_nodes[p] - gll_nodes[m])
                    for k in range(5):
                        if k != p and k != m:
                            factor = factor * (gll_nodes[a] - gll_nodes[k]) / (gll_nodes[p] - gll_nodes[k])
                    summed = summed + factor
            derivative[a, p] = summed
    return (gll_nodes, gll_weights, derivative)

def time_filter():
    offsets = np.arange(NSAMP) - (NSAMP - 1) / 2.0
    cardinal = np.sin(np.pi * offsets) / (np.pi * offsets)
    values = cardinal * (0.5 + 0.5 * np.cos(np.pi * offsets / (NSAMP / 2.0)))
    return values / np.sum(values)

def lagrange_rows(points, gll_nodes):
    result_rows = []
    for p in range(5):
        value_row = jnp.ones_like(points)
        for m in range(5):
            if m != p:
                scale_term = float(1.0 / (gll_nodes[p] - gll_nodes[m]))
                value_row = value_row * ((points - float(gll_nodes[m])) * scale_term)
        result_rows.append(value_row)
    return jnp.stack(result_rows)

def open_axis(nodal_grid, axis_at, elem_count):
    turned = jnp.moveaxis(nodal_grid, axis_at, -1)
    leading = turned[..., :4 * elem_count].reshape(turned.shape[:-1] + (elem_count, 4))
    trailing = turned[..., 4::4][..., None]
    joined = jnp.concatenate([leading, trailing], axis=-1)
    return jnp.moveaxis(joined, (-2, -1), (axis_at, axis_at + 1))

def fold_axis(pieces, axis_at, elem_count):
    turned = jnp.moveaxis(pieces, (axis_at, axis_at + 1), (-2, -1))
    widths = [(0, 0)] * (turned.ndim - 2)
    leading = jnp.pad(turned[..., :4], widths + [(0, 1), (0, 0)])
    trailing = jnp.pad(turned[..., 4], widths + [(1, 0)])
    leading = leading.at[..., 0].add(trailing)
    flat_view = leading.reshape(turned.shape[:-2] + (4 * (elem_count + 1),))[..., :4 * elem_count + 1]
    return jnp.moveaxis(flat_view, -1, axis_at)

def to_elements(nodal_grid, ex_count, ey_count, ez_count):
    opened = open_axis(nodal_grid, 1, ex_count)
    opened = open_axis(opened, 3, ey_count)
    opened = open_axis(opened, 5, ez_count)
    opened = jnp.transpose(opened, (0, 2, 4, 6, 1, 3, 5))
    return opened.reshape(opened.shape[:4] + (ex_count * ey_count * ez_count,))

def from_elements(pieces, ex_count, ey_count, ez_count):
    shaped = pieces.reshape(pieces.shape[:4] + (ex_count, ey_count, ez_count))
    shaped = jnp.transpose(shaped, (0, 4, 1, 5, 2, 6, 3))
    shaped = fold_axis(shaped, 5, ez_count)
    shaped = fold_axis(shaped, 3, ey_count)
    return fold_axis(shaped, 1, ex_count)

def element_terms(adj_parts, fwd_parts, shear_vals, lame_vals, derivative, gll_weights):
    diff_matrix = jnp.asarray(derivative, jnp.float32)

    def gradient(pieces):
        along_x = jnp.einsum('ap,ipbce->iabce', diff_matrix, pieces, precision=highest)
        along_y = jnp.einsum('bp,iapce->iabce', diff_matrix, pieces, precision=highest)
        along_z = jnp.einsum('cp,iabpe->iabce', diff_matrix, pieces, precision=highest)
        return jnp.stack([along_x, along_y, along_z], axis=1)
    unit_tensor = jnp.eye(3, dtype=jnp.float32)[:, :, None, None, None, None]
    adj_grad = gradient(adj_parts)
    fwd_grad = gradient(fwd_parts)
    adj_strain = 0.5 * (adj_grad + jnp.swapaxes(adj_grad, 0, 1))
    fwd_strain = 0.5 * (fwd_grad + jnp.swapaxes(fwd_grad, 0, 1))
    adj_trace = adj_strain[0, 0] + adj_strain[1, 1] + adj_strain[2, 2]
    fwd_trace = fwd_strain[0, 0] + fwd_strain[1, 1] + fwd_strain[2, 2]
    stress = 2.0 * shear_vals * adj_strain + unit_tensor * (lame_vals * adj_trace)
    weight_vec = np.asarray(gll_weights)
    cubature = jnp.asarray(weight_vec[:, None, None] * weight_vec[None, :, None] * weight_vec[None, None, :], jnp.float32)[..., None]
    weighted = stress * cubature
    divergence = jnp.einsum('pa,ipbce->iabce', diff_matrix, weighted[:, 0], precision=highest)
    divergence = divergence + jnp.einsum('pb,iapce->iabce', diff_matrix, weighted[:, 1], precision=highest)
    divergence = divergence + jnp.einsum('pc,iabpe->iabce', diff_matrix, weighted[:, 2], precision=highest)
    adj_dev = adj_strain - unit_tensor * (adj_trace / 3.0)
    fwd_dev = fwd_strain - unit_tensor * (fwd_trace / 3.0)
    shear_term = 2.0 * shear_vals * lax.optimization_barrier(jnp.sum(adj_dev * fwd_dev, axis=(0, 1)))
    bulk_term = (lame_vals + 2.0 / 3.0 * shear_vals) * adj_trace * fwd_trace
    return (divergence, shear_term, bulk_term)

def source_rows(records, element_ids, elem_total, gll_nodes):
    record_count = records.shape[1]
    block_rows = 4096 if record_count % 4096 == 0 else record_count

    def accumulate(running, turn_index):
        record_block = lax.dynamic_slice_in_dim(records, turn_index * block_rows, block_rows, 1)
        owners = lax.dynamic_slice_in_dim(element_ids, turn_index * block_rows, block_rows, 0)
        basis_x = lagrange_rows(record_block[3], gll_nodes)
        basis_y = lagrange_rows(record_block[4], gll_nodes)
        basis_z = lagrange_rows(record_block[5], gll_nodes)
        spread = (basis_x[:, None, None, :] * basis_y[None, :, None, :] * basis_z[None, None, :, :]).reshape(125, block_rows)
        nodal_force = (record_block[0:3, None, :] * spread[None]).reshape(375, block_rows)
        return (running.at[owners].add(nodal_force.T), None)
    running, _ = lax.scan(accumulate, jnp.zeros((elem_total, 375), jnp.float32), jnp.arange(record_count // block_rows, dtype=jnp.int32))
    return running

def reference(adj_disp, adj_veloc, fwd_disp, inv_mass, shear_mod, lame_mod, kernel_mu, kernel_kappa, chan_window, chan_dir, chan_local, chan_part, chan_elem):
    gll_nodes, gll_weights, derivative = gll_tables()
    filter_row = jnp.asarray(time_filter(), jnp.float32)[None, :]
    strength = jnp.dot(filter_row, chan_window, precision=highest, preferred_element_type=jnp.float32)
    records = jnp.concatenate([strength * chan_dir, chan_local], axis=0)
    owners = chan_part[:, 0] * ELEM_DEV + chan_elem
    source_all = source_rows(records, owners, ELEM_TOTAL, gll_nodes)
    source_slabs = source_all.reshape(N_GX, N_GY, EX, EY, EZ, 375)
    both_fields = jnp.concatenate([adj_disp, fwd_disp], axis=0)
    padded = jnp.pad(both_fields, ((0, 0), (0, 1), (0, 1), (0, 1)))
    rows_y = EY * N_GY

    def regroup(term):
        shaped = term.reshape(125, EX, N_GY, EY, EZ)
        return jnp.transpose(shaped, (0, 2, 1, 3, 4)).reshape(125, N_GY * ELEM_DEV)

    def slab_terms(slab_index):
        nodal = lax.dynamic_slice_in_dim(padded, slab_index * (4 * EX), 4 * EX + 1, 1)
        element_parts = to_elements(nodal, EX, rows_y, EZ)
        shear_vals = lax.dynamic_slice_in_dim(shear_mod, slab_index * EX, EX, 0).reshape(-1)
        lame_vals = lax.dynamic_slice_in_dim(lame_mod, slab_index * EX, EX, 0).reshape(-1)
        divergence, shear_term, bulk_term = element_terms(element_parts[:3], element_parts[3:], shear_vals, lame_vals, derivative, gll_weights)
        source_here = lax.dynamic_index_in_dim(source_slabs, slab_index, 0, keepdims=False)
        source_here = jnp.transpose(source_here, (4, 1, 0, 2, 3)).reshape(3, 5, 5, 5, EX * rows_y * EZ)
        force_grid = from_elements(source_here - divergence, EX, rows_y, EZ)
        return (force_grid[:, :4 * EX, :NYG, :NZ], force_grid[:, 4 * EX, :NYG, :NZ], regroup(shear_term), regroup(bulk_term))
    mains, extras, shear_inc, bulk_inc = lax.map(slab_terms, jnp.arange(N_GX, dtype=jnp.int32))
    assembled = jnp.moveaxis(mains, 0, 1)
    assembled = assembled.at[:, 1:, 0].add(jnp.moveaxis(extras[:-1], 0, 1))
    assembled = assembled.reshape(3, NXG, NYG, NZ)
    adj_veloc_new = adj_veloc + time_step * (inv_mass[None] * assembled)
    adj_disp_new = adj_disp + time_step * adj_veloc_new
    kernel_mu_new = kernel_mu + time_step * jnp.moveaxis(shear_inc, 0, 1).reshape(125, ELEM_TOTAL)
    kernel_kappa_new = kernel_kappa + time_step * jnp.moveaxis(bulk_inc, 0, 1).reshape(125, ELEM_TOTAL)
    return (adj_disp_new, adj_veloc_new, kernel_mu_new, kernel_kappa_new)
```

```python
import jax
import jax.numpy as jnp
import numpy as np
from jax import lax
from jax.experimental import pallas as pl
from jax.experimental.pallas import tpu as pltpu
from jax.sharding import PartitionSpec as P

NSAMP = 16
time_step = 0.05
f32, bf16, i32 = jnp.float32, jnp.bfloat16, jnp.int32

EX, EY, EZ = 2, 4, 32
NCH = 8192
NDEV = 128
CAP = 128
ELEMS = EX * EY * EZ
LIMIT = 56 * 1024 * 1024


def gll_tables():
    gll_nodes = np.array([-1.0, -np.sqrt(3.0 / 7.0), 0.0, np.sqrt(3.0 / 7.0), 1.0])
    gll_weights = np.array([0.1, 49.0 / 90.0, 32.0 / 45.0, 49.0 / 90.0, 0.1])
    derivative = np.zeros((5, 5))
    for a in range(5):
        for p in range(5):
            summed = 0.0
            for m in range(5):
                if m != p:
                    factor = 1.0 / (gll_nodes[p] - gll_nodes[m])
                    for k in range(5):
                        if k != p and k != m:
                            factor = (
                                factor
                                * (gll_nodes[a] - gll_nodes[k])
                                / (gll_nodes[p] - gll_nodes[k])
                            )
                    summed = summed + factor
            derivative[a, p] = summed
    return (gll_nodes, gll_weights, derivative)


def time_filter():
    offsets = np.arange(NSAMP) - (NSAMP - 1) / 2.0
    cardinal = np.sin(np.pi * offsets) / (np.pi * offsets)
    values = cardinal * (0.5 + 0.5 * np.cos(np.pi * offsets / (NSAMP / 2.0)))
    return values / np.sum(values)


nodes, weights, deriv = gll_tables()


def halves(matrix):
    matrix = np.asarray(matrix, np.float32)
    top = matrix.astype(jnp.bfloat16)
    low = (matrix - top.astype(np.float32)).astype(jnp.bfloat16)
    return top, low


def padded_row(c, a, b):
    return c * 40 + a * 8 + b


def build_tables():
    select = np.zeros((EY * 128, 5 * 128), np.float32)
    for ey in range(EY):
        for c in range(5):
            for ez in range(EZ):
                if 4 * ez + c < 128:
                    select[ey * 128 + 4 * ez + c, c * 128 + ey * 32 + ez] = 1.0
    grad = np.zeros((384, 208))
    div = np.zeros((208, 384))
    for a in range(5):
        for b in range(5):
            for c in range(5):
                row = 25 * a + 5 * b + c
                for p in range(5):
                    grad[row, padded_row(c, p, b)] += deriv[a, p]
                    grad[128 + row, padded_row(c, a, p)] += deriv[b, p]
                    grad[256 + row, padded_row(p, a, b)] += deriv[c, p]
                    out = padded_row(c, a, b)
                    div[out, 25 * p + 5 * b + c] += (
                        deriv[p, a] * weights[p] * weights[b] * weights[c]
                    )
                    div[out, 128 + 25 * a + 5 * p + c] += (
                        deriv[p, b] * weights[a] * weights[p] * weights[c]
                    )
                    div[out, 256 + 25 * a + 5 * b + p] += (
                        deriv[p, c] * weights[a] * weights[b] * weights[p]
                    )
    place = np.zeros((608, 384), np.float32)
    for i in range(3):
        for a in range(5):
            for b in range(5):
                for c in range(5):
                    bc = 5 * b + c
                    at = (i * 5 + a) * 24 + bc if bc < 24 else 360 + i * 5 + a
                    place[i * 200 + padded_row(c, a, b), at] = 1.0
    upper = np.zeros((256, 384), np.float32)
    upper[:, :256] = np.arange(256)[:, None] < np.arange(256)[None, :]
    upper[:, 256:] = 1.0
    return select, grad, div, place, upper


SELECT, GRAD, DIV, PLACE, UPPER = build_tables()


def shifted(x, axis, by):
    peers = lax.axis_size(axis)
    pairs = [(i, i + by) for i in range(peers) if 0 <= i + by < peers]
    return lax.ppermute(x, axis, pairs)


def dot(x, y):
    return jnp.dot(x, y, preferred_element_type=f32)


def dot_nt(x, y):
    return lax.dot_general(x, y, (((1,), (1,)), ((), ())), preferred_element_type=f32)


def split2(x):
    top = x.astype(bf16)
    return top, (x - top.astype(f32)).astype(bf16)


PACK_CHUNK = 512


def pack_kernel(
    win_ref, dir_ref, loc_ref, part_ref, elem_ref, coef_ref, upper_ref, out_ref, key_ref, a_ref, acc_ref
):
    upper = upper_ref[...]

    def rank_step(at, base):
        span = pl.ds(pl.multiple_of(at * 256, 256), 256)
        target = part_ref[:, span]
        same = lax.broadcasted_iota(i32, (NDEV, 256), 0) == target
        running = dot(jnp.where(same, 1.0, 0.0).astype(bf16), upper)
        before = running[:, :256] + jnp.concatenate([base, base], axis=1)
        rank = jnp.sum(jnp.where(same, before, 0.0), axis=0, keepdims=True)
        key_ref[:, span] = rank.astype(i32) + (target >> 6) * CAP
        return base + running[:, 256:]

    lax.fori_loop(0, NCH // 256, rank_step, jnp.zeros((NDEV, 128), f32), unroll=4)
    acc_ref[...] = jnp.zeros_like(acc_ref)
    coef = coef_ref[:, 0:1]

    def fill_step(at, carry):
        span = pl.ds(pl.multiple_of(at * PACK_CHUNK, PACK_CHUNK), PACK_CHUNK)
        strength = jnp.sum(win_ref[:, span] * coef, axis=0, keepdims=True)
        force = strength * dir_ref[:, span]
        where_at = loc_ref[:, span]
        force_low = force - force.astype(bf16).astype(f32)
        where_low = where_at - where_at.astype(bf16).astype(f32)
        elem = elem_ref[:, span].astype(f32)
        rows = [force[k : k + 1] for k in range(3)] + [where_at[k : k + 1] for k in range(3)]
        rows += [force_low[k : k + 1] for k in range(3)] + [where_low[k : k + 1] for k in range(3)]
        rows += [elem]
        mask = lax.broadcasted_iota(i32, (64, PACK_CHUNK), 0) == (part_ref[:, span] & 63)
        for k, row in enumerate(rows):
            a_ref[k * 64 : (k + 1) * 64, :] = jnp.where(mask, row, 0.0).astype(bf16)
        slot = lax.broadcasted_iota(i32, (256, PACK_CHUNK), 0) == key_ref[:, span]
        acc_ref[...] += dot_nt(a_ref[...], jnp.where(slot, 1.0, 0.0).astype(bf16))
        return carry

    lax.fori_loop(0, NCH // PACK_CHUNK, fill_step, 0)
    for half in range(2):
        lanes = slice(half * 128, (half + 1) * 128)
        for v in range(6):
            out_ref[pl.ds(half * 512 + v, 64, stride=8), :] = (
                acc_ref[v * 64 : (v + 1) * 64, lanes] + acc_ref[(6 + v) * 64 : (7 + v) * 64, lanes]
            )
        out_ref[pl.ds(half * 512 + 6, 64, stride=8), :] = acc_ref[12 * 64 : 13 * 64, lanes]
        out_ref[pl.ds(half * 512 + 7, 64, stride=8), :] = jnp.zeros((64, 128), f32)


def pack(chan_window, chan_dir, chan_local, part_row, elem_row):
    coef = np.tile(time_filter().astype(np.float32)[:, None], (1, 128))
    return pl.pallas_call(
        pack_kernel,
        out_shape=jax.ShapeDtypeStruct((NDEV * 8, 128), f32),
        scratch_shapes=[
            pltpu.VMEM((1, NCH), i32),
            pltpu.VMEM((13 * 64, PACK_CHUNK), bf16),
            pltpu.VMEM((13 * 64, 256), f32),
        ],
        compiler_params=pltpu.CompilerParams(vmem_limit_bytes=LIMIT),
        cost_estimate=pl.CostEstimate(
            flops=5 * 10**9, bytes_accessed=1500000, transcendentals=0
        ),
        name="pack",
    )(chan_window, chan_dir, chan_local, part_row, elem_row, jnp.asarray(coef), jnp.asarray(UPPER, bf16))


def element_kernel(
    adj_ref,
    fwd_ref,
    strike_ref,
    dip_ref,
    shear_ref,
    lame_ref,
    mu_ref,
    kappa_ref,
    select_ref,
    grad_ref,
    div_ref,
    mu_out,
    kappa_out,
    force_out,
    n_ref,
    x_ref,
    u_ref,
    g_ref,
    t_ref,
):
    for f in range(6):
        source = adj_ref if f < 3 else fwd_ref
        for x in range(9):
            base = (f * 9 + x) * 24
            if x < 8:
                n_ref[base : base + 16, :] = source[f % 3, x]
            else:
                n_ref[base : base + 16, :] = strike_ref[f]
            n_ref[base + 16 : base + 24, :] = jnp.zeros((8, 128), f32)
            n_ref[base + 16 : base + 17, :] = dip_ref[f, x : x + 1, :]
    for f in range(6):
        for ex in range(EX):
            for a in range(5):
                for ey in range(EY):
                    base = (f * 9 + 4 * ex + a) * 24 + 4 * ey
                    at = (f * 2 + ex) * 40 + a * 8
                    x_ref[at : at + 8, ey * 128 : (ey + 1) * 128] = n_ref[base : base + 8, :]
    whole = x_ref[...]
    top, rest = whole.astype(bf16), None
    rest = whole - top.astype(f32)
    mid = rest.astype(bf16)
    low = (rest - mid.astype(f32)).astype(bf16)
    select = select_ref[...]
    opened = (dot(low, select) + dot(mid, select)) + dot(top, select)
    for block in range(12):
        for c in range(5):
            u_ref[c * 40 : (c + 1) * 40, block * 128 : (block + 1) * 128] = opened[
                block * 40 : (block + 1) * 40, c * 128 : (c + 1) * 128
            ]
    u_ref[200:208, :] = jnp.zeros((8, 1536), f32)
    top, low = split2(u_ref[...])
    both = dot(grad_ref[...], top)
    g_ref[...] = both[:384] + (both[384:] + dot(grad_ref[:384, :], low))
    for ex in range(EX):
        lanes = slice(ex * 128, (ex + 1) * 128)
        shear = shear_ref[:, lanes]
        lame = lame_ref[:, lanes]
        bulk = lame + 2.0 / 3.0 * shear
        for tile in range(16):
            rows = slice(tile * 8, tile * 8 + 8)

            def grad(f, i, j):
                block = (f * 3 + i) * 2 + ex
                return g_ref[j * 128 + tile * 8 : j * 128 + tile * 8 + 8, block * 128 : (block + 1) * 128]

            strains = []
            for f in range(2):
                strain = {}
                for i in range(3):
                    strain[i, i] = grad(f, i, i)
                    for j in range(i):
                        strain[i, j] = 0.5 * (grad(f, i, j) + grad(f, j, i))
                        strain[j, i] = strain[i, j]
                strains.append(strain)
            adj, fwd = strains
            adj_trace = adj[0, 0] + adj[1, 1] + adj[2, 2]
            fwd_trace = fwd[0, 0] + fwd[1, 1] + fwd[2, 2]
            twice = 2.0 * shear
            pressure = lame * adj_trace
            for i in range(3):
                for j in range(3):
                    value = twice * adj[i, j]
                    if i == j:
                        value = value + pressure
                    block = i * 2 + ex
                    t_ref[j * 128 + tile * 8 : j * 128 + tile * 8 + 8, block * 128 : (block + 1) * 128] = value
            traces = adj_trace * fwd_trace
            product = (
                adj[0, 0] * fwd[0, 0] + adj[1, 1] * fwd[1, 1] + adj[2, 2] * fwd[2, 2]
            ) - traces * (1.0 / 3.0)
            product = product + 2.0 * (
                adj[1, 0] * fwd[1, 0] + adj[2, 0] * fwd[2, 0] + adj[2, 1] * fwd[2, 1]
            )
            count = 8 if tile < 15 else 5
            rows = slice(tile * 8, tile * 8 + count)
            mu_out[rows, lanes] = mu_ref[rows, lanes] + (time_step * twice * product)[:count]
            kappa_out[rows, lanes] = kappa_ref[rows, lanes] + (time_step * bulk * traces)[:count]
    top, low = split2(t_ref[...])
    both = dot(div_ref[...], top)
    result = both[:208] + (both[208:] + dot(div_ref[:208, :], low))
    for i in range(3):
        force_out[i * 200 : (i + 1) * 200, :] = result[:200, i * 256 : (i + 1) * 256]


def element_terms(adj, fwd, strike, dip, shear, lame, mu, kappa):
    grad = np.concatenate(halves(GRAD), axis=0)
    div = np.concatenate(halves(DIV), axis=0)
    return pl.pallas_call(
        element_kernel,
        out_shape=[
            jax.ShapeDtypeStruct((125, ELEMS), f32),
            jax.ShapeDtypeStruct((125, ELEMS), f32),
            jax.ShapeDtypeStruct((600, ELEMS), f32),
        ],
        scratch_shapes=[
            pltpu.VMEM((6 * 9 * 24, 128), f32),
            pltpu.VMEM((480, 512), f32),
            pltpu.VMEM((208, 1536), f32),
            pltpu.VMEM((384, 1536), f32),
            pltpu.VMEM((384, 768), f32),
        ],
        compiler_params=pltpu.CompilerParams(vmem_limit_bytes=LIMIT),
        cost_estimate=pl.CostEstimate(
            flops=5 * 10**9, bytes_accessed=5000000, transcendentals=0
        ),
        name="element_terms",
    )(adj, fwd, strike, dip, shear, lame, mu, kappa, jnp.asarray(SELECT, bf16), jnp.asarray(grad), jnp.asarray(div))


def source_kernel(
    inc_ref,
    div_ref,
    place_ref,
    back_ref,
    main_out,
    dip_out,
    strike_out,
    gx_ref,
    yz_ref,
    a_ref,
    b_ref,
    acc_ref,
    z_ref,
    f_ref,
):
    acc_ref[...] = jnp.zeros_like(acc_ref)

    def basis(points):
        gaps = [points - float(np.float32(nodes[m])) for m in range(5)]
        result = []
        for p in range(5):
            scale = 1.0
            value = None
            for m in range(5):
                if m != p:
                    scale = scale / (nodes[p] - nodes[m])
                    value = gaps[m] if value is None else value * gaps[m]
            result.append(value * float(scale))
        return result

    def step(at, carry):
        base = pl.multiple_of(at * 64, 64)
        values = [inc_ref[pl.ds(base + v, 8, stride=8), :] for v in range(7)]
        lx, ly, lz = basis(values[3]), basis(values[4]), basis(values[5])
        for i in range(3):
            for a in range(5):
                gx_ref[pl.ds(i * 5 + a, 8, stride=16), :] = values[i] * lx[a]
        gx_ref[pl.ds(15, 8, stride=16), :] = jnp.zeros((8, 128), f32)
        for b in range(5):
            for c in range(5):
                yz_ref[pl.ds(b * 5 + c, 8, stride=32), :] = ly[b] * lz[c]
        index = values[6].astype(i32)
        for s in range(8):
            yz = yz_ref[s * 32 : s * 32 + 24, :]
            parts = [gx_ref[s * 16 + k : s * 16 + k + 1, :] * yz for k in range(15)]
            parts.append(gx_ref[s * 16 : s * 16 + 16, :] * yz_ref[s * 32 + 24 : s * 32 + 25, :])
            parts.append(jnp.zeros((8, 128), f32))
            whole = jnp.concatenate(parts, axis=0)
            top, low = split2(whole)
            lanes = slice(s * 128, (s + 1) * 128)
            a_ref[0:384, lanes] = top
            a_ref[384:768, lanes] = low
            here = lax.broadcasted_iota(i32, (ELEMS, 128), 0) == index[s : s + 1, :]
            b_ref[:, lanes] = jnp.where(here, 1.0, 0.0).astype(bf16)
        acc_ref[...] += dot_nt(a_ref[...], b_ref[...])
        return carry

    lax.fori_loop(0, 16, step, 0)
    source = acc_ref[0:384, :] + acc_ref[384:768, :]
    top, low = split2(source)
    place = place_ref[...]
    placed = dot(place, top) + dot(place, low)
    for i in range(3):
        for c in range(5):
            at = i * 200 + c * 40
            block = placed[at : at + 40, :] - div_ref[at : at + 40, :]
            for ex in range(EX):
                to = (i * 2 + ex) * 40
                z_ref[to : to + 40, c * 128 : (c + 1) * 128] = block[:, ex * 128 : (ex + 1) * 128]
    top, low = split2(z_ref[...])
    back = back_ref[...]
    nodal = dot(top, back) + dot(low, back)
    f_ref[...] = jnp.zeros_like(f_ref)
    for i in range(3):
        for ex in range(EX):
            for a in range(5):
                at = (i * 2 + ex) * 40 + a * 8
                for ey in range(EY):
                    to = (i * 9 + 4 * ex + a) * 24 + 4 * ey
                    f_ref[to : to + 8, :] += nodal[at : at + 8, ey * 128 : (ey + 1) * 128]
    for i in range(3):
        for x in range(9):
            at = (i * 9 + x) * 24
            if x < 8:
                main_out[i, x] = f_ref[at : at + 16, :]
            else:
                strike_out[i] = f_ref[at : at + 16, :]
            dip_out[i, x : x + 1, :] = f_ref[at + 16 : at + 17, :]


def source_forces(incoming, divergence):
    return pl.pallas_call(
        source_kernel,
        out_shape=[
            jax.ShapeDtypeStruct((3, 8, 16, 128), f32),
            jax.ShapeDtypeStruct((3, 9, 128), f32),
            jax.ShapeDtypeStruct((3, 16, 128), f32),
        ],
        scratch_shapes=[
            pltpu.VMEM((128, 128), f32),
            pltpu.VMEM((256, 128), f32),
            pltpu.VMEM((768, 1024), bf16),
            pltpu.VMEM((256, 1024), bf16),
            pltpu.VMEM((768, 256), f32),
            pltpu.VMEM((240, 640), f32),
            pltpu.VMEM((3 * 9 * 24, 128), f32),
        ],
        compiler_params=pltpu.CompilerParams(vmem_limit_bytes=LIMIT),
        cost_estimate=pl.CostEstimate(
            flops=7 * 10**9, bytes_accessed=2500000, transcendentals=0
        ),
        name="source_forces",
    )(incoming, divergence, jnp.asarray(PLACE, bf16), jnp.asarray(SELECT.T.copy(), bf16))


def update_kernel(
    disp_ref, veloc_ref, mass_ref, force_ref, dip_ref, strike_ref, disp_out, veloc_out, f_ref
):
    f_ref[...] = force_ref[...]
    for i in range(3):
        for x in range(8):
            f_ref[i, x, 0:1, :] += dip_ref[i, x : x + 1, :]
        f_ref[i, 0] += strike_ref[i]
    for i in range(3):
        veloc = veloc_ref[i] + time_step * (mass_ref[...] * f_ref[i])
        veloc_out[i] = veloc
        disp_out[i] = disp_ref[i] + time_step * veloc


def update(disp, veloc, mass, force, dip, strike):
    shape = jax.ShapeDtypeStruct((3, 8, 16, 128), f32)
    return pl.pallas_call(
        update_kernel,
        out_shape=[shape, shape],
        scratch_shapes=[pltpu.VMEM((3, 8, 16, 128), f32)],
        name="update",
    )(disp, veloc, mass, force, dip, strike)


def local(
    adj_disp,
    adj_veloc,
    fwd_disp,
    inv_mass,
    shear_mod,
    lame_mod,
    kernel_mu,
    kernel_kappa,
    chan_window,
    chan_dir,
    chan_local,
    chan_part,
    chan_elem,
):
    outgoing = pack(
        chan_window, chan_dir, chan_local, chan_part.reshape(1, NCH), chan_elem.reshape(1, NCH)
    )
    incoming = lax.all_to_all(
        outgoing.reshape(NDEV, 8, 128), ("gx", "gy"), split_axis=0, concat_axis=0, tiled=True
    )
    first = jnp.concatenate([adj_disp[:, 0], fwd_disp[:, 0]], axis=0)
    strike = shifted(first, "gx", -1)
    edge = jnp.concatenate([adj_disp[:, :, 0], fwd_disp[:, :, 0]], axis=0)
    dip = shifted(jnp.concatenate([edge, strike[:, 0:1]], axis=1), "gy", -1)
    mu_new, kappa_new, divergence = element_terms(
        adj_disp,
        fwd_disp,
        strike,
        dip,
        shear_mod.reshape(1, ELEMS),
        lame_mod.reshape(1, ELEMS),
        kernel_mu,
        kernel_kappa,
    )
    force, dip_force, strike_force = source_forces(incoming.reshape(NDEV * 8, 128), divergence)
    back_dip = shifted(dip_force, "gy", 1)
    back_strike = shifted(strike_force.at[:, 0].add(back_dip[:, 8]), "gx", 1)
    disp_new, veloc_new = update(adj_disp, adj_veloc, inv_mass, force, back_dip, back_strike)
    return (disp_new, veloc_new, mu_new, kappa_new)


def solution(mesh):
    return jax.shard_map(
        local,
        mesh=mesh,
        in_specs=(
            P(None, "gx", "gy", None),
            P(None, "gx", "gy", None),
            P(None, "gx", "gy", None),
            P("gx", "gy", None),
            P("gx", "gy", None),
            P("gx", "gy", None),
            P(None, ("gx", "gy")),
            P(None, ("gx", "gy")),
            P(None, ("gx", "gy")),
            P(None, ("gx", "gy")),
            P(None, ("gx", "gy")),
            P(("gx", "gy"), None),
            P(("gx", "gy")),
        ),
        out_specs=(
            P(None, "gx", "gy", None),
            P(None, "gx", "gy", None),
            P(None, ("gx", "gy")),
            P(None, ("gx", "gy")),
        ),
        check_vma=False,
    )
```

```python
import jax
import jax.numpy as jnp
import numpy as np
from jax import lax
from jax.experimental import pallas as pl
from jax.experimental.pallas import tpu as pltpu
from jax.sharding import PartitionSpec as P

NSAMP = 16
time_step = 0.05
f32, bf16, i32 = jnp.float32, jnp.bfloat16, jnp.int32

EX, EY, EZ = 2, 4, 32
NCH = 8192
NDEV = 128
CAP = 128
ELEMS = EX * EY * EZ
LIMIT = 56 * 1024 * 1024
LOW_LIMIT = 24 * 1024 * 1024


def gll_tables():
    gll_nodes = np.array([-1.0, -np.sqrt(3.0 / 7.0), 0.0, np.sqrt(3.0 / 7.0), 1.0])
    gll_weights = np.array([0.1, 49.0 / 90.0, 32.0 / 45.0, 49.0 / 90.0, 0.1])
    derivative = np.zeros((5, 5))
    for a in range(5):
        for p in range(5):
            summed = 0.0
            for m in range(5):
                if m != p:
                    factor = 1.0 / (gll_nodes[p] - gll_nodes[m])
                    for k in range(5):
                        if k != p and k != m:
                            factor = (
                                factor
                                * (gll_nodes[a] - gll_nodes[k])
                                / (gll_nodes[p] - gll_nodes[k])
                            )
                    summed = summed + factor
            derivative[a, p] = summed
    return (gll_nodes, gll_weights, derivative)


def time_filter():
    offsets = np.arange(NSAMP) - (NSAMP - 1) / 2.0
    cardinal = np.sin(np.pi * offsets) / (np.pi * offsets)
    values = cardinal * (0.5 + 0.5 * np.cos(np.pi * offsets / (NSAMP / 2.0)))
    return values / np.sum(values)


nodes, weights, deriv = gll_tables()


def halves(matrix):
    matrix = np.asarray(matrix, np.float32)
    top = matrix.astype(jnp.bfloat16)
    low = (matrix - top.astype(np.float32)).astype(jnp.bfloat16)
    return top, low


def padded_row(c, a, b):
    return c * 40 + a * 8 + b


def build_tables():
    select = np.zeros((EY * 128, 5 * 128), np.float32)
    for ey in range(EY):
        for c in range(5):
            for ez in range(EZ):
                if 4 * ez + c < 128:
                    select[ey * 128 + 4 * ez + c, c * 128 + ey * 32 + ez] = 1.0
    grad = np.zeros((384, 208))
    div = np.zeros((208, 384))
    for a in range(5):
        for b in range(5):
            for c in range(5):
                row = 25 * a + 5 * b + c
                for p in range(5):
                    grad[row, padded_row(c, p, b)] += deriv[a, p]
                    grad[128 + row, padded_row(c, a, p)] += deriv[b, p]
                    grad[256 + row, padded_row(p, a, b)] += deriv[c, p]
                    out = padded_row(c, a, b)
                    div[out, 25 * p + 5 * b + c] += (
                        deriv[p, a] * weights[p] * weights[b] * weights[c]
                    )
                    div[out, 128 + 25 * a + 5 * p + c] += (
                        deriv[p, b] * weights[a] * weights[p] * weights[c]
                    )
                    div[out, 256 + 25 * a + 5 * b + p] += (
                        deriv[p, c] * weights[a] * weights[b] * weights[p]
                    )
    place = np.zeros((608, 384), np.float32)
    for i in range(3):
        for a in range(5):
            for b in range(5):
                for c in range(5):
                    bc = 5 * b + c
                    at = (i * 5 + a) * 24 + bc if bc < 24 else 360 + i * 5 + a
                    place[i * 200 + padded_row(c, a, b), at] = 1.0
    upper = np.asarray(np.arange(256)[:, None] <= np.arange(256)[None, :], np.float32)
    return select, grad, div, place, upper


SELECT, GRAD, DIV, PLACE, UPPER = build_tables()


def shifted(x, step_x, step_y):
    size_x, size_y = lax.axis_size("gx"), lax.axis_size("gy")
    if step_y == 0:
        return lax.ppermute(x, "gx", [(i, (i + step_x) % size_x) for i in range(size_x)])
    if step_x == 0:
        return lax.ppermute(x, "gy", [(i, (i + step_y) % size_y) for i in range(size_y)])
    pairs = [
        (i * size_y + j, (i + step_x) % size_x * size_y + (j + step_y) % size_y)
        for i in range(size_x)
        for j in range(size_y)
    ]
    return lax.ppermute(x, ("gx", "gy"), pairs)


def dot(x, y):
    return jnp.dot(x, y, preferred_element_type=f32)


def dot_nt(x, y):
    return lax.dot_general(x, y, (((1,), (1,)), ((), ())), preferred_element_type=f32)


def split2(x):
    top = x.astype(bf16)
    return top, (x - top.astype(f32)).astype(bf16)


def low_row(row, rows):
    tile = jnp.broadcast_to(row, (16, row.shape[1])).astype(bf16)
    return jnp.concatenate([tile] * (rows // 16), axis=0)


def one_hot(row, rows):
    numbers = lax.broadcasted_iota(i32, (rows, row.shape[1]), 0).astype(f32).astype(bf16)
    return jnp.where(numbers == low_row(row, rows), jnp.ones((), bf16), jnp.zeros((), bf16))


PACK_CHUNK = 2048
PACK_UNROLL = 2


def pack_kernel(
    win_hbm,
    dir_hbm,
    loc_hbm,
    part_hbm,
    elem_hbm,
    coef_hbm,
    upper_hbm,
    adj_hbm,
    fwd_hbm,
    out_ref,
    edge_ref,
    acc_ref,
    win_ref,
    dir_ref,
    loc_ref,
    part_ref,
    elem_ref,
    coef_ref,
    upper_ref,
    adj_ref,
    fwd_ref,
    sems,
    *a_refs,
):
    edge = pl.ds(0, 8)
    pairs = [
        (upper_hbm, upper_ref),
        (part_hbm, part_ref),
        (win_hbm, win_ref),
        (coef_hbm, coef_ref),
        (dir_hbm, dir_ref),
        (loc_hbm, loc_ref),
        (elem_hbm, elem_ref),
        (adj_hbm.at[:, :, edge, :], adj_ref),
        (fwd_hbm.at[:, :, edge, :], fwd_ref),
    ]
    copies = [pltpu.make_async_copy(a, b, sems.at[k]) for k, (a, b) in enumerate(pairs)]
    for copy in copies:
        copy.start()
    acc_ref[...] = jnp.zeros_like(acc_ref)
    for copy in copies[:7]:
        copy.wait()
    upper = upper_ref[...]
    coef = coef_ref[:, 0:1]

    def fill(at, base, a_ref):
        blocks = PACK_CHUNK // 256
        targets, same = [], []
        for block in range(blocks):
            span = pl.ds(pl.multiple_of(at * PACK_CHUNK + block * 256, 256), 256)
            targets.append(part_ref[:, span])
            same.append(lax.broadcasted_iota(i32, (NDEV, 256), 0) == targets[block])
        hits = jnp.concatenate([jnp.where(hit, 1.0, 0.0).astype(bf16) for hit in same], axis=0)
        running = dot(hits, upper)
        keys = []
        for block in range(blocks):
            upto = running[block * NDEV : (block + 1) * NDEV, :]
            rank = jnp.sum(jnp.where(same[block], upto + base, 0.0), axis=0, keepdims=True)
            keys.append(rank + ((targets[block] >> 6) * CAP - 1).astype(f32))
            base = base + upto[:, 255:256]
        key = jnp.concatenate(keys, axis=1)
        span = pl.ds(pl.multiple_of(at * PACK_CHUNK, PACK_CHUNK), PACK_CHUNK)
        strength = jnp.sum(win_ref[:, span] * coef, axis=0, keepdims=True)
        force = strength * dir_ref[:, span]
        where_at = loc_ref[:, span]
        force_low = force - force.astype(bf16).astype(f32)
        where_low = where_at - where_at.astype(bf16).astype(f32)
        elem = elem_ref[:, span].astype(f32)
        rows = [force[k : k + 1] for k in range(3)] + [where_at[k : k + 1] for k in range(3)]
        rows += [force_low[k : k + 1] for k in range(3)] + [where_low[k : k + 1] for k in range(3)]
        rows += [elem]
        mask = one_hot((part_ref[:, span] & 63).astype(f32), 64)
        for k, row in enumerate(rows):
            a_ref[k * 64 : (k + 1) * 64, :] = mask * low_row(row, 64)
        acc_ref[...] += dot_nt(a_ref[...], one_hot(key, 256))
        return base

    def step(at, base):
        for k in range(PACK_UNROLL):
            base = fill(at * PACK_UNROLL + k, base, a_refs[k])
        return base

    lax.fori_loop(0, NCH // PACK_CHUNK // PACK_UNROLL, step, jnp.zeros((NDEV, 1), f32))
    for half in range(2):
        lanes = slice(half * 128, (half + 1) * 128)
        for v in range(6):
            out_ref[pl.ds(half * 512 + v, 64, stride=8), :] = (
                acc_ref[v * 64 : (v + 1) * 64, lanes] + acc_ref[(6 + v) * 64 : (7 + v) * 64, lanes]
            )
        out_ref[pl.ds(half * 512 + 6, 64, stride=8), :] = acc_ref[12 * 64 : 13 * 64, lanes]
        out_ref[pl.ds(half * 512 + 7, 64, stride=8), :] = jnp.zeros((64, 128), f32)
    for copy in copies[7:]:
        copy.wait()
    for f in range(6):
        source = adj_ref if f < 3 else fwd_ref
        for x in range(8):
            edge_ref[f, x : x + 1, :] = source[f % 3, x, 0:1, :]


def pack(chan_window, chan_dir, chan_local, part_row, elem_row, adj, fwd):
    coef = np.tile(time_filter().astype(np.float32)[:, None], (1, 128))
    hbm = pl.BlockSpec(memory_space=pl.ANY)
    return pl.pallas_call(
        pack_kernel,
        out_shape=[
            jax.ShapeDtypeStruct((NDEV * 8, 128), f32),
            jax.ShapeDtypeStruct((6, 8, 128), f32),
        ],
        in_specs=[hbm] * 9,
        scratch_shapes=[
            pltpu.VMEM((13 * 64, 256), f32),
            pltpu.VMEM((NSAMP, NCH), f32),
            pltpu.VMEM((3, NCH), f32),
            pltpu.VMEM((3, NCH), f32),
            pltpu.VMEM((1, NCH), i32),
            pltpu.VMEM((1, NCH), i32),
            pltpu.VMEM((NSAMP, 128), f32),
            pltpu.VMEM((256, 256), bf16),
            pltpu.VMEM((3, 8, 8, 128), f32),
            pltpu.VMEM((3, 8, 8, 128), f32),
            pltpu.SemaphoreType.DMA((9,)),
        ]
        + [pltpu.VMEM((13 * 64, PACK_CHUNK), bf16)] * PACK_UNROLL,
        compiler_params=pltpu.CompilerParams(vmem_limit_bytes=LIMIT),
        cost_estimate=pl.CostEstimate(
            flops=5 * 10**9, bytes_accessed=1500000, transcendentals=0
        ),
        name="pack",
    )(
        chan_window,
        chan_dir,
        chan_local,
        part_row,
        elem_row,
        jnp.asarray(coef),
        jnp.asarray(UPPER, bf16),
        adj,
        fwd,
    )


def element_kernel(
    adj_ref,
    fwd_ref,
    strike_ref,
    dip_ref,
    shear_ref,
    lame_ref,
    mu_ref,
    kappa_ref,
    select_ref,
    grad_ref,
    div_ref,
    mu_out,
    kappa_out,
    force_out,
    n_ref,
    x_ref,
    u_ref,
    g_ref,
    t_ref,
):
    in_x = lax.axis_index("gx") < lax.axis_size("gx") - 1
    in_y = lax.axis_index("gy") < lax.axis_size("gy") - 1
    for f in range(6):
        source = adj_ref if f < 3 else fwd_ref
        for x in range(9):
            base = (f * 9 + x) * 24
            inside = in_y
            if x < 8:
                n_ref[base : base + 16, :] = source[f % 3, x]
            else:
                n_ref[base : base + 16, :] = jnp.where(in_x, strike_ref[f], 0.0)
                inside = in_x & in_y
            n_ref[base + 16 : base + 24, :] = jnp.zeros((8, 128), f32)
            n_ref[base + 16 : base + 17, :] = jnp.where(inside, dip_ref[f, x : x + 1, :], 0.0)
    for f in range(6):
        for ex in range(EX):
            for a in range(5):
                for ey in range(EY):
                    base = (f * 9 + 4 * ex + a) * 24 + 4 * ey
                    at = (f * 2 + ex) * 40 + a * 8
                    x_ref[at : at + 8, ey * 128 : (ey + 1) * 128] = n_ref[base : base + 8, :]
    whole = x_ref[...]
    top, rest = whole.astype(bf16), None
    rest = whole - top.astype(f32)
    mid = rest.astype(bf16)
    low = (rest - mid.astype(f32)).astype(bf16)
    select = select_ref[...]
    opened = (dot(low, select) + dot(mid, select)) + dot(top, select)
    for block in range(12):
        for c in range(5):
            u_ref[c * 40 : (c + 1) * 40, block * 128 : (block + 1) * 128] = opened[
                block * 40 : (block + 1) * 40, c * 128 : (c + 1) * 128
            ]
    u_ref[200:208, :] = jnp.zeros((8, 1536), f32)
    top, low = split2(u_ref[...])
    both = dot(grad_ref[...], top)
    g_ref[...] = both[:384] + (both[384:] + dot(grad_ref[:384, :], low))
    for ex in range(EX):
        lanes = slice(ex * 128, (ex + 1) * 128)
        shear = jnp.concatenate([shear_ref[ex, ey : ey + 1, :] for ey in range(EY)], axis=1)
        lame = jnp.concatenate([lame_ref[ex, ey : ey + 1, :] for ey in range(EY)], axis=1)
        bulk = lame + 2.0 / 3.0 * shear
        for tile in range(16):
            rows = slice(tile * 8, tile * 8 + 8)

            def grad(f, i, j):
                block = (f * 3 + i) * 2 + ex
                return g_ref[j * 128 + tile * 8 : j * 128 + tile * 8 + 8, block * 128 : (block + 1) * 128]

            strains = []
            for f in range(2):
                strain = {}
                for i in range(3):
                    strain[i, i] = grad(f, i, i)
                    for j in range(i):
                        strain[i, j] = 0.5 * (grad(f, i, j) + grad(f, j, i))
                        strain[j, i] = strain[i, j]
                strains.append(strain)
            adj, fwd = strains
            adj_trace = adj[0, 0] + adj[1, 1] + adj[2, 2]
            fwd_trace = fwd[0, 0] + fwd[1, 1] + fwd[2, 2]
            twice = 2.0 * shear
            pressure = lame * adj_trace
            for i in range(3):
                for j in range(3):
                    value = twice * adj[i, j]
                    if i == j:
                        value = value + pressure
                    block = i * 2 + ex
                    t_ref[j * 128 + tile * 8 : j * 128 + tile * 8 + 8, block * 128 : (block + 1) * 128] = value
            traces = adj_trace * fwd_trace
            product = (
                adj[0, 0] * fwd[0, 0] + adj[1, 1] * fwd[1, 1] + adj[2, 2] * fwd[2, 2]
            ) - traces * (1.0 / 3.0)
            product = product + 2.0 * (
                adj[1, 0] * fwd[1, 0] + adj[2, 0] * fwd[2, 0] + adj[2, 1] * fwd[2, 1]
            )
            count = 8 if tile < 15 else 5
            rows = slice(tile * 8, tile * 8 + count)
            mu_out[rows, lanes] = mu_ref[rows, lanes] + (time_step * twice * product)[:count]
            kappa_out[rows, lanes] = kappa_ref[rows, lanes] + (time_step * bulk * traces)[:count]
    top, low = split2(t_ref[...])
    both = dot(div_ref[...], top)
    result = both[:208] + (both[208:] + dot(div_ref[:208, :], low))
    for i in range(3):
        force_out[i * 200 : (i + 1) * 200, :] = result[:200, i * 256 : (i + 1) * 256]


def element_terms(adj, fwd, strike, dip, shear, lame, mu, kappa):
    grad = np.concatenate(halves(GRAD), axis=0)
    div = np.concatenate(halves(DIV), axis=0)
    return pl.pallas_call(
        element_kernel,
        out_shape=[
            jax.ShapeDtypeStruct((125, ELEMS), f32),
            jax.ShapeDtypeStruct((125, ELEMS), f32),
            jax.ShapeDtypeStruct((600, ELEMS), f32),
        ],
        scratch_shapes=[
            pltpu.VMEM((6 * 9 * 24, 128), f32),
            pltpu.VMEM((480, 512), f32),
            pltpu.VMEM((208, 1536), f32),
            pltpu.VMEM((384, 1536), f32),
            pltpu.VMEM((384, 768), f32),
        ],
        compiler_params=pltpu.CompilerParams(vmem_limit_bytes=LOW_LIMIT),
        cost_estimate=pl.CostEstimate(
            flops=5 * 10**9, bytes_accessed=5000000, transcendentals=0
        ),
        name="element_terms",
    )(adj, fwd, strike, dip, shear, lame, mu, kappa, jnp.asarray(SELECT, bf16), jnp.asarray(grad), jnp.asarray(div))


GROUP = 8
SPREAD_UNROLL = 4


def source_kernel(
    inc_ref,
    div_ref,
    place_ref,
    back_ref,
    main_out,
    dip_out,
    strike_out,
    corner_out,
    acc_ref,
    z_ref,
    f_ref,
    *parts_refs,
):
    turns = 128 // GROUP // SPREAD_UNROLL
    acc_ref[...] = jnp.zeros_like(acc_ref)

    def basis(points):
        gaps = [points - float(np.float32(nodes[m])) for m in range(5)]
        result = []
        for p in range(5):
            scale = 1.0
            value = None
            for m in range(5):
                if m != p:
                    scale = scale / (nodes[p] - nodes[m])
                    value = gaps[m] if value is None else value * gaps[m]
            result.append(value * float(scale))
        return result

    def spread(at, gx_ref, yz_ref, a_ref, b_ref):
        for sub in range(GROUP // 8):
            base = pl.multiple_of(at * (GROUP * 8) + sub * 64, 64)
            values = [inc_ref[pl.ds(base + v, 8, stride=8), :] for v in range(7)]
            lx, ly, lz = basis(values[3]), basis(values[4]), basis(values[5])
            for i in range(3):
                for a in range(5):
                    gx_ref[pl.ds(sub * 128 + i * 5 + a, 8, stride=16), :] = values[i] * lx[a]
            gx_ref[pl.ds(sub * 128 + 15, 8, stride=16), :] = jnp.zeros((8, 128), f32)
            for b in range(5):
                for c in range(5):
                    yz_ref[pl.ds(sub * 256 + b * 5 + c, 8, stride=32), :] = ly[b] * lz[c]
            index = values[6]
            for k in range(8):
                s = sub * 8 + k
                lanes = slice(s * 128, (s + 1) * 128)
                b_ref[:, lanes] = one_hot(index[k : k + 1, :], ELEMS)
                yz = yz_ref[s * 32 : s * 32 + 24, :]
                last = yz_ref[s * 32 + 24 : s * 32 + 25, :]
                for pair in range(8):
                    row = s * 16 + 2 * pair
                    parts = [gx_ref[row : row + 1, :] * yz]
                    if pair < 7:
                        parts += [gx_ref[row + 1 : row + 2, :] * yz]
                    else:
                        parts += [gx_ref[s * 16 : s * 16 + 16, :] * last, jnp.zeros((8, 128), f32)]
                    top, low = split2(jnp.concatenate(parts, axis=0))
                    a_ref[pair * 48 : pair * 48 + 48, lanes] = top
                    a_ref[384 + pair * 48 : 384 + pair * 48 + 48, lanes] = low

    def gather(gx_ref, yz_ref, a_ref, b_ref):
        acc_ref[...] += dot_nt(a_ref[...], b_ref[...])

    sets = [parts_refs[4 * k : 4 * k + 4] for k in range(SPREAD_UNROLL)]

    def step(at, carry):
        for k in range(SPREAD_UNROLL):
            spread(at * SPREAD_UNROLL + k, *sets[k])
            gather(*sets[k])
        return carry

    lax.fori_loop(0, turns, step, 0)
    source = acc_ref[0:384, :] + acc_ref[384:768, :]
    top, low = split2(source)
    place = place_ref[...]
    placed = dot(place, top) + dot(place, low)
    for i in range(3):
        for c in range(5):
            at = i * 200 + c * 40
            block = placed[at : at + 40, :] - div_ref[at : at + 40, :]
            for ex in range(EX):
                to = (i * 2 + ex) * 40
                z_ref[to : to + 40, c * 128 : (c + 1) * 128] = block[:, ex * 128 : (ex + 1) * 128]
    top, low = split2(z_ref[...])
    back = back_ref[...]
    nodal = dot(top, back) + dot(low, back)
    f_ref[...] = jnp.zeros_like(f_ref)
    for i in range(3):
        for ex in range(EX):
            for a in range(5):
                at = (i * 2 + ex) * 40 + a * 8
                for ey in range(EY):
                    to = (i * 9 + 4 * ex + a) * 24 + 4 * ey
                    f_ref[to : to + 8, :] += nodal[at : at + 8, ey * 128 : (ey + 1) * 128]
    for i in range(3):
        for x in range(9):
            at = (i * 9 + x) * 24
            if x < 8:
                main_out[i, x] = f_ref[at : at + 16, :]
                dip_out[i, x : x + 1, :] = f_ref[at + 16 : at + 17, :]
            else:
                strike_out[i] = f_ref[at : at + 16, :]
                corner_out[i : i + 1, :] = f_ref[at + 16 : at + 17, :]


def source_forces(incoming, divergence):
    return pl.pallas_call(
        source_kernel,
        out_shape=[
            jax.ShapeDtypeStruct((3, 8, 16, 128), f32),
            jax.ShapeDtypeStruct((3, 8, 128), f32),
            jax.ShapeDtypeStruct((3, 16, 128), f32),
            jax.ShapeDtypeStruct((3, 128), f32),
        ],
        scratch_shapes=[
            pltpu.VMEM((768, 256), f32),
            pltpu.VMEM((240, 640), f32),
            pltpu.VMEM((3 * 9 * 24, 128), f32),
        ]
        + [
            pltpu.VMEM((GROUP * 16, 128), f32),
            pltpu.VMEM((GROUP * 32, 128), f32),
            pltpu.VMEM((768, GROUP * 128), bf16),
            pltpu.VMEM((256, GROUP * 128), bf16),
        ]
        * SPREAD_UNROLL,
        compiler_params=pltpu.CompilerParams(vmem_limit_bytes=LOW_LIMIT),
        cost_estimate=pl.CostEstimate(
            flops=7 * 10**9, bytes_accessed=2500000, transcendentals=0
        ),
        name="source_forces",
    )(incoming, divergence, jnp.asarray(PLACE, bf16), jnp.asarray(SELECT.T.copy(), bf16))


def update_kernel(
    disp_ref, veloc_ref, mass_ref, force_ref, dip_ref, strike_ref, corner_ref, disp_out, veloc_out, f_ref
):
    in_x = lax.axis_index("gx") > 0
    in_y = lax.axis_index("gy") > 0
    f_ref[...] = force_ref[...]
    for i in range(3):
        for x in range(8):
            f_ref[i, x, 0:1, :] += jnp.where(in_y, dip_ref[i, x : x + 1, :], 0.0)
        f_ref[i, 0] += jnp.where(in_x, strike_ref[i], 0.0)
        f_ref[i, 0, 0:1, :] += jnp.where(in_x & in_y, corner_ref[i : i + 1, :], 0.0)
    for i in range(3):
        veloc = veloc_ref[i] + time_step * (mass_ref[...] * f_ref[i])
        veloc_out[i] = veloc
        disp_out[i] = disp_ref[i] + time_step * veloc


def update(disp, veloc, mass, force, dip, strike, corner):
    shape = jax.ShapeDtypeStruct((3, 8, 16, 128), f32)
    return pl.pallas_call(
        update_kernel,
        out_shape=[shape, shape],
        scratch_shapes=[pltpu.VMEM((3, 8, 16, 128), f32)],
        compiler_params=pltpu.CompilerParams(vmem_limit_bytes=8 * 1024 * 1024),
        name="update",
    )(disp, veloc, mass, force, dip, strike, corner)


def local(
    adj_disp,
    adj_veloc,
    fwd_disp,
    inv_mass,
    shear_mod,
    lame_mod,
    kernel_mu,
    kernel_kappa,
    chan_window,
    chan_dir,
    chan_local,
    chan_part,
    chan_elem,
):
    first = jnp.concatenate([adj_disp[:, 0], fwd_disp[:, 0]], axis=0)
    strike = shifted(first, -1, 0)
    outgoing, edge = pack(
        chan_window,
        chan_dir,
        chan_local,
        chan_part.reshape(1, NCH),
        chan_elem.reshape(1, NCH),
        adj_disp,
        fwd_disp,
    )
    incoming = lax.all_to_all(
        outgoing.reshape(NDEV, 8, 128), ("gx", "gy"), split_axis=0, concat_axis=0, tiled=True
    )
    dip = shifted(jnp.concatenate([edge, strike[:, 0:1]], axis=1), 0, -1)
    mu_new, kappa_new, divergence = element_terms(
        adj_disp, fwd_disp, strike, dip, shear_mod, lame_mod, kernel_mu, kernel_kappa
    )
    force, dip_force, strike_force, corner_force = source_forces(
        incoming.reshape(NDEV * 8, 128), divergence
    )
    disp_new, veloc_new = update(
        adj_disp,
        adj_veloc,
        inv_mass,
        force,
        shifted(dip_force, 0, 1),
        shifted(strike_force, 1, 0),
        shifted(corner_force, 1, 1),
    )
    return (disp_new, veloc_new, mu_new, kappa_new)


def solution(mesh):
    return jax.shard_map(
        local,
        mesh=mesh,
        in_specs=(
            P(None, "gx", "gy", None),
            P(None, "gx", "gy", None),
            P(None, "gx", "gy", None),
            P("gx", "gy", None),
            P("gx", "gy", None),
            P("gx", "gy", None),
            P(None, ("gx", "gy")),
            P(None, ("gx", "gy")),
            P(None, ("gx", "gy")),
            P(None, ("gx", "gy")),
            P(None, ("gx", "gy")),
            P(("gx", "gy"), None),
            P(("gx", "gy")),
        ),
        out_specs=(
            P(None, "gx", "gy", None),
            P(None, "gx", "gy", None),
            P(None, ("gx", "gy")),
            P(None, ("gx", "gy")),
        ),
        check_vma=False,
    )
```

```python
import jax
import jax.numpy as jnp
import numpy as np
from jax import lax
from jax.experimental import pallas as pl
from jax.experimental.pallas import tpu as pltpu
from jax.sharding import PartitionSpec as P

NSAMP = 16
time_step = 0.05
f32, bf16, i32 = jnp.float32, jnp.bfloat16, jnp.int32

EX, EY, EZ = 2, 4, 32
NCH = 8192
NDEV = 128
CAP = 128
ELEMS = EX * EY * EZ
LIMIT = 56 * 1024 * 1024
LOW_LIMIT = 24 * 1024 * 1024


def gll_tables():
    gll_nodes = np.array([-1.0, -np.sqrt(3.0 / 7.0), 0.0, np.sqrt(3.0 / 7.0), 1.0])
    gll_weights = np.array([0.1, 49.0 / 90.0, 32.0 / 45.0, 49.0 / 90.0, 0.1])
    derivative = np.zeros((5, 5))
    for a in range(5):
        for p in range(5):
            summed = 0.0
            for m in range(5):
                if m != p:
                    factor = 1.0 / (gll_nodes[p] - gll_nodes[m])
                    for k in range(5):
                        if k != p and k != m:
                            factor = (
                                factor
                                * (gll_nodes[a] - gll_nodes[k])
                                / (gll_nodes[p] - gll_nodes[k])
                            )
                    summed = summed + factor
            derivative[a, p] = summed
    return (gll_nodes, gll_weights, derivative)


def time_filter():
    offsets = np.arange(NSAMP) - (NSAMP - 1) / 2.0
    cardinal = np.sin(np.pi * offsets) / (np.pi * offsets)
    values = cardinal * (0.5 + 0.5 * np.cos(np.pi * offsets / (NSAMP / 2.0)))
    return values / np.sum(values)


nodes, weights, deriv = gll_tables()


def halves(matrix):
    matrix = np.asarray(matrix, np.float32)
    top = matrix.astype(jnp.bfloat16)
    low = (matrix - top.astype(np.float32)).astype(jnp.bfloat16)
    return top, low


def padded_row(c, a, b):
    return c * 40 + a * 8 + b


def build_tables():
    select = np.zeros((EY * 128, 5 * 128), np.float32)
    for ey in range(EY):
        for c in range(5):
            for ez in range(EZ):
                if 4 * ez + c < 128:
                    select[ey * 128 + 4 * ez + c, c * 128 + ey * 32 + ez] = 1.0
    grad = np.zeros((384, 208))
    div = np.zeros((128, 384))
    for a in range(5):
        for b in range(5):
            for c in range(5):
                row = 25 * a + 5 * b + c
                for p in range(5):
                    grad[row, padded_row(c, p, b)] += deriv[a, p]
                    grad[128 + row, padded_row(c, a, p)] += deriv[b, p]
                    grad[256 + row, padded_row(p, a, b)] += deriv[c, p]
                    bc = 5 * b + c
                    out = a * 24 + bc if bc < 24 else 120 + a
                    div[out, 25 * p + 5 * b + c] += (
                        deriv[p, a] * weights[p] * weights[b] * weights[c]
                    )
                    div[out, 128 + 25 * a + 5 * p + c] += (
                        deriv[p, b] * weights[a] * weights[p] * weights[c]
                    )
                    div[out, 256 + 25 * a + 5 * b + p] += (
                        deriv[p, c] * weights[a] * weights[b] * weights[p]
                    )
    place = np.zeros((608, 384), np.float32)
    for i in range(3):
        for a in range(5):
            for b in range(5):
                for c in range(5):
                    bc = 5 * b + c
                    at = (i * 5 + a) * 24 + bc if bc < 24 else 360 + i * 5 + a
                    place[i * 200 + padded_row(c, a, b), at] = 1.0
    upper = np.asarray(np.arange(256)[:, None] <= np.arange(256)[None, :], np.float32)
    return select, grad, div, place, upper


SELECT, GRAD, DIV, PLACE, UPPER = build_tables()


def shifted(x, step_x, step_y):
    size_x, size_y = lax.axis_size("gx"), lax.axis_size("gy")
    if step_y == 0:
        return lax.ppermute(x, "gx", [(i, (i + step_x) % size_x) for i in range(size_x)])
    if step_x == 0:
        return lax.ppermute(x, "gy", [(i, (i + step_y) % size_y) for i in range(size_y)])
    pairs = [
        (i * size_y + j, (i + step_x) % size_x * size_y + (j + step_y) % size_y)
        for i in range(size_x)
        for j in range(size_y)
    ]
    return lax.ppermute(x, ("gx", "gy"), pairs)


def dot(x, y):
    return jnp.dot(x, y, preferred_element_type=f32)


def dot_nt(x, y):
    return lax.dot_general(x, y, (((1,), (1,)), ((), ())), preferred_element_type=f32)


def split2(x):
    top = x.astype(bf16)
    return top, (x - top.astype(f32)).astype(bf16)


def low_row(row, rows):
    tile = jnp.broadcast_to(row, (16, row.shape[1])).astype(bf16)
    return jnp.concatenate([tile] * (rows // 16), axis=0)


def one_hot(row, rows):
    numbers = lax.broadcasted_iota(i32, (rows, row.shape[1]), 0).astype(f32).astype(bf16)
    return jnp.where(numbers == low_row(row, rows), jnp.ones((), bf16), jnp.zeros((), bf16))


PACK_CHUNK = 2048
PACK_UNROLL = 2


def pack_kernel(
    win_hbm,
    dir_hbm,
    loc_hbm,
    part_hbm,
    elem_hbm,
    coef_hbm,
    upper_hbm,
    adj_hbm,
    fwd_hbm,
    out_ref,
    edge_ref,
    acc_ref,
    win_ref,
    dir_ref,
    loc_ref,
    part_ref,
    elem_ref,
    coef_ref,
    upper_ref,
    adj_ref,
    fwd_ref,
    sems,
    *a_refs,
):
    edge = pl.ds(0, 8)
    pairs = [
        (upper_hbm, upper_ref),
        (part_hbm, part_ref),
        (win_hbm, win_ref),
        (coef_hbm, coef_ref),
        (dir_hbm, dir_ref),
        (loc_hbm, loc_ref),
        (elem_hbm, elem_ref),
        (adj_hbm.at[:, :, edge, :], adj_ref),
        (fwd_hbm.at[:, :, edge, :], fwd_ref),
    ]
    copies = [pltpu.make_async_copy(a, b, sems.at[k]) for k, (a, b) in enumerate(pairs)]
    for copy in copies:
        copy.start()
    acc_ref[...] = jnp.zeros_like(acc_ref)
    for copy in copies[:7]:
        copy.wait()
    upper = upper_ref[...]
    coef = coef_ref[:, 0:1]

    def fill(at, base, a_ref):
        blocks = PACK_CHUNK // 256
        targets, same = [], []
        for block in range(blocks):
            span = pl.ds(pl.multiple_of(at * PACK_CHUNK + block * 256, 256), 256)
            targets.append(part_ref[:, span])
            same.append(lax.broadcasted_iota(i32, (NDEV, 256), 0) == targets[block])
        hits = jnp.concatenate([jnp.where(hit, 1.0, 0.0).astype(bf16) for hit in same], axis=0)
        running = dot(hits, upper)
        keys = []
        for block in range(blocks):
            upto = running[block * NDEV : (block + 1) * NDEV, :]
            rank = jnp.sum(jnp.where(same[block], upto + base, 0.0), axis=0, keepdims=True)
            keys.append(rank + ((targets[block] >> 6) * CAP - 1).astype(f32))
            base = base + upto[:, 255:256]
        key = jnp.concatenate(keys, axis=1)
        span = pl.ds(pl.multiple_of(at * PACK_CHUNK, PACK_CHUNK), PACK_CHUNK)
        strength = jnp.sum(win_ref[:, span] * coef, axis=0, keepdims=True)
        force = strength * dir_ref[:, span]
        where_at = loc_ref[:, span]
        force_low = force - force.astype(bf16).astype(f32)
        where_low = where_at - where_at.astype(bf16).astype(f32)
        elem = elem_ref[:, span].astype(f32)
        rows = [force[k : k + 1] for k in range(3)] + [where_at[k : k + 1] for k in range(3)]
        rows += [force_low[k : k + 1] for k in range(3)] + [where_low[k : k + 1] for k in range(3)]
        rows += [elem]
        mask = one_hot((part_ref[:, span] & 63).astype(f32), 64)
        for k, row in enumerate(rows):
            a_ref[k * 64 : (k + 1) * 64, :] = mask * low_row(row, 64)
        acc_ref[...] += dot_nt(a_ref[...], one_hot(key, 256))
        return base

    def step(at, base):
        for k in range(PACK_UNROLL):
            base = fill(at * PACK_UNROLL + k, base, a_refs[k])
        return base

    lax.fori_loop(0, NCH // PACK_CHUNK // PACK_UNROLL, step, jnp.zeros((NDEV, 1), f32))
    for half in range(2):
        lanes = slice(half * 128, (half + 1) * 128)
        for v in range(6):
            out_ref[pl.ds(half * 512 + v, 64, stride=8), :] = (
                acc_ref[v * 64 : (v + 1) * 64, lanes] + acc_ref[(6 + v) * 64 : (7 + v) * 64, lanes]
            )
        out_ref[pl.ds(half * 512 + 6, 64, stride=8), :] = acc_ref[12 * 64 : 13 * 64, lanes]
        out_ref[pl.ds(half * 512 + 7, 64, stride=8), :] = jnp.zeros((64, 128), f32)
    for copy in copies[7:]:
        copy.wait()
    for f in range(6):
        source = adj_ref if f < 3 else fwd_ref
        for x in range(8):
            edge_ref[f, x : x + 1, :] = source[f % 3, x, 0:1, :]


def pack(chan_window, chan_dir, chan_local, part_row, elem_row, adj, fwd):
    coef = np.tile(time_filter().astype(np.float32)[:, None], (1, 128))
    hbm = pl.BlockSpec(memory_space=pl.ANY)
    return pl.pallas_call(
        pack_kernel,
        out_shape=[
            jax.ShapeDtypeStruct((NDEV * 8, 128), f32),
            jax.ShapeDtypeStruct((6, 8, 128), f32),
        ],
        in_specs=[hbm] * 9,
        scratch_shapes=[
            pltpu.VMEM((13 * 64, 256), f32),
            pltpu.VMEM((NSAMP, NCH), f32),
            pltpu.VMEM((3, NCH), f32),
            pltpu.VMEM((3, NCH), f32),
            pltpu.VMEM((1, NCH), i32),
            pltpu.VMEM((1, NCH), i32),
            pltpu.VMEM((NSAMP, 128), f32),
            pltpu.VMEM((256, 256), bf16),
            pltpu.VMEM((3, 8, 8, 128), f32),
            pltpu.VMEM((3, 8, 8, 128), f32),
            pltpu.SemaphoreType.DMA((9,)),
        ]
        + [pltpu.VMEM((13 * 64, PACK_CHUNK), bf16)] * PACK_UNROLL,
        compiler_params=pltpu.CompilerParams(vmem_limit_bytes=LIMIT),
        cost_estimate=pl.CostEstimate(
            flops=5 * 10**9, bytes_accessed=1500000, transcendentals=0
        ),
        name="pack",
    )(
        chan_window,
        chan_dir,
        chan_local,
        part_row,
        elem_row,
        jnp.asarray(coef),
        jnp.asarray(UPPER, bf16),
        adj,
        fwd,
    )


def select_matrix():
    lane = lax.broadcasted_iota(i32, (1, 640), 1)
    at = 4 * (lane & 31) + (lane >> 7)
    row = (lane >> 5) & 3
    parts = [one_hot(jnp.where(row == ey, at, 255).astype(f32), 128) for ey in range(EY)]
    return jnp.concatenate(parts, axis=0)


def element_kernel(
    adj_ref,
    fwd_ref,
    strike_ref,
    dip_ref,
    shear_ref,
    lame_ref,
    mu_ref,
    kappa_ref,
    table_ref,
    mu_out,
    kappa_out,
    force_out,
    n_ref,
    x_ref,
    u_ref,
    g_ref,
    t_ref,
):
    in_x = lax.axis_index("gx") < lax.axis_size("gx") - 1
    in_y = lax.axis_index("gy") < lax.axis_size("gy") - 1
    for f in range(6):
        source = adj_ref if f < 3 else fwd_ref
        for x in range(9):
            base = (f * 9 + x) * 24
            inside = in_y
            if x < 8:
                n_ref[base : base + 16, :] = source[f % 3, x]
            else:
                n_ref[base : base + 16, :] = jnp.where(in_x, strike_ref[f], 0.0)
                inside = in_x & in_y
            n_ref[base + 16 : base + 24, :] = jnp.zeros((8, 128), f32)
            n_ref[base + 16 : base + 17, :] = jnp.where(inside, dip_ref[f, x : x + 1, :], 0.0)
    for f in range(6):
        for ex in range(EX):
            for a in range(5):
                for ey in range(EY):
                    base = (f * 9 + 4 * ex + a) * 24 + 4 * ey
                    at = (f * 2 + ex) * 40 + a * 8
                    x_ref[at : at + 8, ey * 128 : (ey + 1) * 128] = n_ref[base : base + 8, :]
    whole = x_ref[...]
    top, rest = whole.astype(bf16), None
    rest = whole - top.astype(f32)
    mid = rest.astype(bf16)
    low = (rest - mid.astype(f32)).astype(bf16)
    select = select_matrix()
    opened = (dot(low, select) + dot(mid, select)) + dot(top, select)
    for block in range(12):
        for c in range(5):
            u_ref[c * 40 : (c + 1) * 40, block * 128 : (block + 1) * 128] = opened[
                block * 40 : (block + 1) * 40, c * 128 : (c + 1) * 128
            ]
    u_ref[200:208, :] = jnp.zeros((8, 1536), f32)
    top, low = split2(u_ref[...])
    both = dot(table_ref[0:768, 0:208], top)
    g_ref[...] = both[:384] + (both[384:] + dot(table_ref[0:384, 0:208], low))
    for ex in range(EX):
        lanes = slice(ex * 128, (ex + 1) * 128)
        shear = jnp.concatenate([shear_ref[ex, ey : ey + 1, :] for ey in range(EY)], axis=1)
        lame = jnp.concatenate([lame_ref[ex, ey : ey + 1, :] for ey in range(EY)], axis=1)
        bulk = lame + 2.0 / 3.0 * shear
        for tile in range(16):
            rows = slice(tile * 8, tile * 8 + 8)

            def grad(f, i, j):
                block = (f * 3 + i) * 2 + ex
                return g_ref[j * 128 + tile * 8 : j * 128 + tile * 8 + 8, block * 128 : (block + 1) * 128]

            strains = []
            for f in range(2):
                strain = {}
                for i in range(3):
                    strain[i, i] = grad(f, i, i)
                    for j in range(i):
                        strain[i, j] = 0.5 * (grad(f, i, j) + grad(f, j, i))
                        strain[j, i] = strain[i, j]
                strains.append(strain)
            adj, fwd = strains
            adj_trace = adj[0, 0] + adj[1, 1] + adj[2, 2]
            fwd_trace = fwd[0, 0] + fwd[1, 1] + fwd[2, 2]
            twice = 2.0 * shear
            pressure = lame * adj_trace
            for i in range(3):
                for j in range(3):
                    value = twice * adj[i, j]
                    if i == j:
                        value = value + pressure
                    block = i * 2 + ex
                    t_ref[j * 128 + tile * 8 : j * 128 + tile * 8 + 8, block * 128 : (block + 1) * 128] = value
            traces = adj_trace * fwd_trace
            product = (
                adj[0, 0] * fwd[0, 0] + adj[1, 1] * fwd[1, 1] + adj[2, 2] * fwd[2, 2]
            ) - traces * (1.0 / 3.0)
            product = product + 2.0 * (
                adj[1, 0] * fwd[1, 0] + adj[2, 0] * fwd[2, 0] + adj[2, 1] * fwd[2, 1]
            )
            count = 8 if tile < 15 else 5
            rows = slice(tile * 8, tile * 8 + count)
            mu_out[rows, lanes] = mu_ref[rows, lanes] + (time_step * twice * product)[:count]
            kappa_out[rows, lanes] = kappa_ref[rows, lanes] + (time_step * bulk * traces)[:count]
    top, low = split2(t_ref[...])
    both = dot(table_ref[768:1024, :], top)
    result = both[:128] + (both[128:] + dot(table_ref[768:896, :], low))
    for i in range(3):
        lanes = slice(i * 256, (i + 1) * 256)
        force_out[i * 120 : (i + 1) * 120, :] = result[:120, lanes]
        force_out[360 + i * 5 : 365 + i * 5, :] = result[120:125, lanes]
    force_out[375:384, :] = jnp.zeros((9, ELEMS), f32)


def element_terms(adj, fwd, strike, dip, shear, lame, mu, kappa):
    grad = np.concatenate(halves(GRAD), axis=0)
    table = np.zeros((1024, 384), grad.dtype)
    table[:768, :208] = grad
    table[768:] = np.concatenate(halves(DIV), axis=0)
    return pl.pallas_call(
        element_kernel,
        out_shape=[
            jax.ShapeDtypeStruct((125, ELEMS), f32),
            jax.ShapeDtypeStruct((125, ELEMS), f32),
            jax.ShapeDtypeStruct((384, ELEMS), f32),
        ],
        scratch_shapes=[
            pltpu.VMEM((6 * 9 * 24, 128), f32),
            pltpu.VMEM((480, 512), f32),
            pltpu.VMEM((208, 1536), f32),
            pltpu.VMEM((384, 1536), f32),
            pltpu.VMEM((384, 768), f32),
        ],
        compiler_params=pltpu.CompilerParams(vmem_limit_bytes=LOW_LIMIT),
        cost_estimate=pl.CostEstimate(
            flops=5 * 10**9, bytes_accessed=5000000, transcendentals=0
        ),
        name="element_terms",
    )(adj, fwd, strike, dip, shear, lame, mu, kappa, jnp.asarray(table))


GROUP = 8
SPREAD_UNROLL = 4


def source_kernel(
    inc_ref,
    div_ref,
    table_ref,
    main_out,
    dip_out,
    strike_out,
    corner_out,
    acc_ref,
    z_ref,
    f_ref,
    *parts_refs,
):
    turns = 128 // GROUP // SPREAD_UNROLL
    acc_ref[...] = jnp.zeros_like(acc_ref)

    def basis(points):
        gaps = [points - float(np.float32(nodes[m])) for m in range(5)]
        result = []
        for p in range(5):
            scale = 1.0
            value = None
            for m in range(5):
                if m != p:
                    scale = scale / (nodes[p] - nodes[m])
                    value = gaps[m] if value is None else value * gaps[m]
            result.append(value * float(scale))
        return result

    def spread(at, gx_ref, yz_ref, a_ref, b_ref):
        for sub in range(GROUP // 8):
            base = pl.multiple_of(at * (GROUP * 8) + sub * 64, 64)
            values = [inc_ref[pl.ds(base + v, 8, stride=8), :] for v in range(7)]
            lx, ly, lz = basis(values[3]), basis(values[4]), basis(values[5])
            for i in range(3):
                for a in range(5):
                    gx_ref[pl.ds(sub * 128 + i * 5 + a, 8, stride=16), :] = values[i] * lx[a]
            gx_ref[pl.ds(sub * 128 + 15, 8, stride=16), :] = jnp.zeros((8, 128), f32)
            for b in range(5):
                for c in range(5):
                    yz_ref[pl.ds(sub * 256 + b * 5 + c, 8, stride=32), :] = ly[b] * lz[c]
            index = values[6]
            for k in range(8):
                s = sub * 8 + k
                lanes = slice(s * 128, (s + 1) * 128)
                b_ref[:, lanes] = one_hot(index[k : k + 1, :], ELEMS)
                yz = yz_ref[s * 32 : s * 32 + 24, :]
                last = yz_ref[s * 32 + 24 : s * 32 + 25, :]
                for pair in range(8):
                    row = s * 16 + 2 * pair
                    parts = [gx_ref[row : row + 1, :] * yz]
                    if pair < 7:
                        parts += [gx_ref[row + 1 : row + 2, :] * yz]
                    else:
                        parts += [gx_ref[s * 16 : s * 16 + 16, :] * last, jnp.zeros((8, 128), f32)]
                    top, low = split2(jnp.concatenate(parts, axis=0))
                    a_ref[pair * 48 : pair * 48 + 48, lanes] = top
                    a_ref[384 + pair * 48 : 384 + pair * 48 + 48, lanes] = low

    def gather(gx_ref, yz_ref, a_ref, b_ref):
        acc_ref[...] += dot_nt(a_ref[...], b_ref[...])

    sets = [parts_refs[4 * k : 4 * k + 4] for k in range(SPREAD_UNROLL)]

    def step(at, carry):
        for k in range(SPREAD_UNROLL):
            spread(at * SPREAD_UNROLL + k, *sets[k])
            gather(*sets[k])
        return carry

    lax.fori_loop(0, turns, step, 0)
    total = acc_ref[0:384, :] + acc_ref[384:768, :] - div_ref[...]
    top, low = split2(total)
    place = table_ref[0:608, 0:384]
    placed = dot(place, top) + dot(place, low)
    for i in range(3):
        for c in range(5):
            at = i * 200 + c * 40
            block = placed[at : at + 40, :]
            for ex in range(EX):
                to = (i * 2 + ex) * 40
                z_ref[to : to + 40, c * 128 : (c + 1) * 128] = block[:, ex * 128 : (ex + 1) * 128]
    top, low = split2(z_ref[...])
    back = table_ref[608:1248, :]
    nodal = dot(top, back) + dot(low, back)
    f_ref[...] = jnp.zeros_like(f_ref)
    for i in range(3):
        for ex in range(EX):
            for a in range(5):
                at = (i * 2 + ex) * 40 + a * 8
                for ey in range(EY):
                    to = (i * 9 + 4 * ex + a) * 24 + 4 * ey
                    f_ref[to : to + 8, :] += nodal[at : at + 8, ey * 128 : (ey + 1) * 128]
    for i in range(3):
        for x in range(9):
            at = (i * 9 + x) * 24
            if x < 8:
                main_out[i, x] = f_ref[at : at + 16, :]
                dip_out[i, x : x + 1, :] = f_ref[at + 16 : at + 17, :]
            else:
                strike_out[i] = f_ref[at : at + 16, :]
                corner_out[i : i + 1, :] = f_ref[at + 16 : at + 17, :]


def source_forces(incoming, divergence):
    table = np.zeros((1248, 512), np.float32)
    table[:608, :384] = PLACE
    table[608:] = SELECT.T
    return pl.pallas_call(
        source_kernel,
        out_shape=[
            jax.ShapeDtypeStruct((3, 8, 16, 128), f32),
            jax.ShapeDtypeStruct((3, 8, 128), f32),
            jax.ShapeDtypeStruct((3, 16, 128), f32),
            jax.ShapeDtypeStruct((3, 128), f32),
        ],
        scratch_shapes=[
            pltpu.VMEM((768, 256), f32),
            pltpu.VMEM((240, 640), f32),
            pltpu.VMEM((3 * 9 * 24, 128), f32),
        ]
        + [
            pltpu.VMEM((GROUP * 16, 128), f32),
            pltpu.VMEM((GROUP * 32, 128), f32),
            pltpu.VMEM((768, GROUP * 128), bf16),
            pltpu.VMEM((256, GROUP * 128), bf16),
        ]
        * SPREAD_UNROLL,
        compiler_params=pltpu.CompilerParams(vmem_limit_bytes=LOW_LIMIT),
        name="source_forces",
    )(incoming, divergence, jnp.asarray(table, bf16))


def update_kernel(
    disp_ref, veloc_ref, mass_ref, force_ref, dip_ref, strike_ref, corner_ref, disp_out, veloc_out, f_ref
):
    in_x = lax.axis_index("gx") > 0
    in_y = lax.axis_index("gy") > 0
    f_ref[...] = force_ref[...]
    for i in range(3):
        for x in range(8):
            f_ref[i, x, 0:1, :] += jnp.where(in_y, dip_ref[i, x : x + 1, :], 0.0)
        f_ref[i, 0] += jnp.where(in_x, strike_ref[i], 0.0)
        f_ref[i, 0, 0:1, :] += jnp.where(in_x & in_y, corner_ref[i : i + 1, :], 0.0)
    for i in range(3):
        veloc = veloc_ref[i] + time_step * (mass_ref[...] * f_ref[i])
        veloc_out[i] = veloc
        disp_out[i] = disp_ref[i] + time_step * veloc


def update(disp, veloc, mass, force, dip, strike, corner):
    shape = jax.ShapeDtypeStruct((3, 8, 16, 128), f32)
    return pl.pallas_call(
        update_kernel,
        out_shape=[shape, shape],
        scratch_shapes=[pltpu.VMEM((3, 8, 16, 128), f32)],
        compiler_params=pltpu.CompilerParams(vmem_limit_bytes=8 * 1024 * 1024),
        name="update",
    )(disp, veloc, mass, force, dip, strike, corner)


def local(
    adj_disp,
    adj_veloc,
    fwd_disp,
    inv_mass,
    shear_mod,
    lame_mod,
    kernel_mu,
    kernel_kappa,
    chan_window,
    chan_dir,
    chan_local,
    chan_part,
    chan_elem,
):
    first = jnp.concatenate([adj_disp[:, 0], fwd_disp[:, 0]], axis=0)
    strike = shifted(first, -1, 0)
    outgoing, edge = pack(
        chan_window,
        chan_dir,
        chan_local,
        chan_part.reshape(1, NCH),
        chan_elem.reshape(1, NCH),
        adj_disp,
        fwd_disp,
    )
    incoming = lax.all_to_all(
        outgoing.reshape(NDEV, 8, 128), ("gx", "gy"), split_axis=0, concat_axis=0, tiled=True
    )
    dip = shifted(jnp.concatenate([edge, strike[:, 0:1]], axis=1), 0, -1)
    mu_new, kappa_new, divergence = element_terms(
        adj_disp, fwd_disp, strike, dip, shear_mod, lame_mod, kernel_mu, kernel_kappa
    )
    force, dip_force, strike_force, corner_force = source_forces(
        incoming.reshape(NDEV * 8, 128), divergence
    )
    disp_new, veloc_new = update(
        adj_disp,
        adj_veloc,
        inv_mass,
        force,
        shifted(dip_force, 0, 1),
        shifted(strike_force, 1, 0),
        shifted(corner_force, 1, 1),
    )
    return (disp_new, veloc_new, mu_new, kappa_new)


def solution(mesh):
    return jax.shard_map(
        local,
        mesh=mesh,
        in_specs=(
            P(None, "gx", "gy", None),
            P(None, "gx", "gy", None),
            P(None, "gx", "gy", None),
            P("gx", "gy", None),
            P("gx", "gy", None),
            P("gx", "gy", None),
            P(None, ("gx", "gy")),
            P(None, ("gx", "gy")),
            P(None, ("gx", "gy")),
            P(None, ("gx", "gy")),
            P(None, ("gx", "gy")),
            P(("gx", "gy"), None),
            P(("gx", "gy")),
        ),
        out_specs=(
            P(None, "gx", "gy", None),
            P(None, "gx", "gy", None),
            P(None, ("gx", "gy")),
            P(None, ("gx", "gy")),
        ),
        check_vma=False,
    )
```

```python
import jax
import jax.numpy as jnp
import numpy as np
from jax import lax
from jax.experimental import pallas as pl
from jax.experimental.pallas import tpu as pltpu
from jax.sharding import PartitionSpec as P

NSAMP = 16
time_step = 0.05
f32, bf16, i32 = jnp.float32, jnp.bfloat16, jnp.int32

EX, EY, EZ = 2, 4, 32
NCH = 8192
NDEV = 128
CAP = 128
ELEMS = EX * EY * EZ
LIMIT = 56 * 1024 * 1024
LOW_LIMIT = 24 * 1024 * 1024


def gll_tables():
    gll_nodes = np.array([-1.0, -np.sqrt(3.0 / 7.0), 0.0, np.sqrt(3.0 / 7.0), 1.0])
    gll_weights = np.array([0.1, 49.0 / 90.0, 32.0 / 45.0, 49.0 / 90.0, 0.1])
    derivative = np.zeros((5, 5))
    for a in range(5):
        for p in range(5):
            summed = 0.0
            for m in range(5):
                if m != p:
                    factor = 1.0 / (gll_nodes[p] - gll_nodes[m])
                    for k in range(5):
                        if k != p and k != m:
                            factor = (
                                factor
                                * (gll_nodes[a] - gll_nodes[k])
                                / (gll_nodes[p] - gll_nodes[k])
                            )
                    summed = summed + factor
            derivative[a, p] = summed
    return (gll_nodes, gll_weights, derivative)


def time_filter():
    offsets = np.arange(NSAMP) - (NSAMP - 1) / 2.0
    cardinal = np.sin(np.pi * offsets) / (np.pi * offsets)
    values = cardinal * (0.5 + 0.5 * np.cos(np.pi * offsets / (NSAMP / 2.0)))
    return values / np.sum(values)


nodes, weights, deriv = gll_tables()


def halves(matrix):
    matrix = np.asarray(matrix, np.float32)
    top = matrix.astype(jnp.bfloat16)
    low = (matrix - top.astype(np.float32)).astype(jnp.bfloat16)
    return top, low


def padded_row(c, a, b):
    return c * 40 + a * 8 + b


def build_tables():
    select = np.zeros((EY * 128, 5 * 128), np.float32)
    for ey in range(EY):
        for c in range(5):
            for ez in range(EZ):
                if 4 * ez + c < 128:
                    select[ey * 128 + 4 * ez + c, c * 128 + ey * 32 + ez] = 1.0
    grad = np.zeros((384, 208))
    div = np.zeros((128, 384))
    for a in range(5):
        for b in range(5):
            for c in range(5):
                row = 25 * a + 5 * b + c
                for p in range(5):
                    grad[row, padded_row(c, p, b)] += deriv[a, p]
                    grad[128 + row, padded_row(c, a, p)] += deriv[b, p]
                    grad[256 + row, padded_row(p, a, b)] += deriv[c, p]
                    bc = 5 * b + c
                    out = a * 24 + bc if bc < 24 else 120 + a
                    div[out, 25 * p + 5 * b + c] += (
                        deriv[p, a] * weights[p] * weights[b] * weights[c]
                    )
                    div[out, 128 + 25 * a + 5 * p + c] += (
                        deriv[p, b] * weights[a] * weights[p] * weights[c]
                    )
                    div[out, 256 + 25 * a + 5 * b + p] += (
                        deriv[p, c] * weights[a] * weights[b] * weights[p]
                    )
    place = np.zeros((608, 384), np.float32)
    for i in range(3):
        for a in range(5):
            for b in range(5):
                for c in range(5):
                    bc = 5 * b + c
                    at = (i * 5 + a) * 24 + bc if bc < 24 else 360 + i * 5 + a
                    place[i * 200 + padded_row(c, a, b), at] = 1.0
    upper = np.asarray(np.arange(256)[:, None] <= np.arange(256)[None, :], np.float32)
    return select, grad, div, place, upper


SELECT, GRAD, DIV, PLACE, UPPER = build_tables()


def shifted(x, step_x, step_y):
    size_x, size_y = lax.axis_size("gx"), lax.axis_size("gy")
    if step_y == 0:
        return lax.ppermute(x, "gx", [(i, (i + step_x) % size_x) for i in range(size_x)])
    if step_x == 0:
        return lax.ppermute(x, "gy", [(i, (i + step_y) % size_y) for i in range(size_y)])
    pairs = [
        (i * size_y + j, (i + step_x) % size_x * size_y + (j + step_y) % size_y)
        for i in range(size_x)
        for j in range(size_y)
    ]
    return lax.ppermute(x, ("gx", "gy"), pairs)


def dot(x, y):
    return jnp.dot(x, y, preferred_element_type=f32)


def dot_nt(x, y):
    return lax.dot_general(x, y, (((1,), (1,)), ((), ())), preferred_element_type=f32)


def split2(x):
    top = x.astype(bf16)
    return top, (x - top.astype(f32)).astype(bf16)


def low_row(row, rows):
    tile = jnp.broadcast_to(row, (16, row.shape[1])).astype(bf16)
    return jnp.concatenate([tile] * (rows // 16), axis=0)


def one_hot(row, rows):
    numbers = lax.broadcasted_iota(i32, (rows, row.shape[1]), 0).astype(f32).astype(bf16)
    return jnp.where(numbers == low_row(row, rows), jnp.ones((), bf16), jnp.zeros((), bf16))


PACK_CHUNK = 2048
PACK_UNROLL = 2


def pack_kernel(
    win_hbm,
    dir_hbm,
    loc_hbm,
    part_hbm,
    elem_hbm,
    coef_hbm,
    upper_hbm,
    adj_hbm,
    fwd_hbm,
    out_ref,
    edge_ref,
    acc_ref,
    win_ref,
    dir_ref,
    loc_ref,
    part_ref,
    elem_ref,
    coef_ref,
    upper_ref,
    adj_ref,
    fwd_ref,
    sems,
    *a_refs,
):
    edge = pl.ds(0, 8)
    pairs = [
        (upper_hbm, upper_ref),
        (part_hbm, part_ref),
        (win_hbm, win_ref),
        (coef_hbm, coef_ref),
        (dir_hbm, dir_ref),
        (loc_hbm, loc_ref),
        (elem_hbm, elem_ref),
        (adj_hbm.at[:, :, edge, :], adj_ref),
        (fwd_hbm.at[:, :, edge, :], fwd_ref),
    ]
    copies = [pltpu.make_async_copy(a, b, sems.at[k]) for k, (a, b) in enumerate(pairs)]
    for copy in copies:
        copy.start()
    acc_ref[...] = jnp.zeros_like(acc_ref)
    for copy in copies[:7]:
        copy.wait()
    upper = upper_ref[...]
    coef = coef_ref[:, 0:1]

    def fill(at, base, a_ref):
        blocks = PACK_CHUNK // 256
        targets, same = [], []
        for block in range(blocks):
            span = pl.ds(pl.multiple_of(at * PACK_CHUNK + block * 256, 256), 256)
            targets.append(part_ref[:, span])
            same.append(lax.broadcasted_iota(i32, (NDEV, 256), 0) == targets[block])
        hits = jnp.concatenate([jnp.where(hit, 1.0, 0.0).astype(bf16) for hit in same], axis=0)
        running = dot(hits, upper)
        keys = []
        for block in range(blocks):
            upto = running[block * NDEV : (block + 1) * NDEV, :]
            rank = jnp.sum(jnp.where(same[block], upto + base, 0.0), axis=0, keepdims=True)
            keys.append(rank + ((targets[block] >> 6) * CAP - 1).astype(f32))
            base = base + upto[:, 255:256]
        key = jnp.concatenate(keys, axis=1)
        span = pl.ds(pl.multiple_of(at * PACK_CHUNK, PACK_CHUNK), PACK_CHUNK)
        strength = jnp.sum(win_ref[:, span] * coef, axis=0, keepdims=True)
        force = strength * dir_ref[:, span]
        where_at = loc_ref[:, span]
        force_low = force - force.astype(bf16).astype(f32)
        where_low = where_at - where_at.astype(bf16).astype(f32)
        elem = elem_ref[:, span].astype(f32)
        rows = [force[k : k + 1] for k in range(3)] + [where_at[k : k + 1] for k in range(3)]
        rows += [force_low[k : k + 1] for k in range(3)] + [where_low[k : k + 1] for k in range(3)]
        rows += [elem]
        mask = one_hot((part_ref[:, span] & 63).astype(f32), 64)
        for k, row in enumerate(rows):
            a_ref[k * 64 : (k + 1) * 64, :] = mask * low_row(row, 64)
        acc_ref[...] += dot_nt(a_ref[...], one_hot(key, 256))
        return base

    def step(at, base):
        for k in range(PACK_UNROLL):
            base = fill(at * PACK_UNROLL + k, base, a_refs[k])
        return base

    lax.fori_loop(0, NCH // PACK_CHUNK // PACK_UNROLL, step, jnp.zeros((NDEV, 1), f32))
    for half in range(2):
        lanes = slice(half * 128, (half + 1) * 128)
        for v in range(6):
            out_ref[pl.ds(half * 512 + v, 64, stride=8), :] = (
                acc_ref[v * 64 : (v + 1) * 64, lanes] + acc_ref[(6 + v) * 64 : (7 + v) * 64, lanes]
            )
        out_ref[pl.ds(half * 512 + 6, 64, stride=8), :] = acc_ref[12 * 64 : 13 * 64, lanes]
        out_ref[pl.ds(half * 512 + 7, 64, stride=8), :] = jnp.zeros((64, 128), f32)
    for copy in copies[7:]:
        copy.wait()
    for f in range(6):
        source = adj_ref if f < 3 else fwd_ref
        for x in range(8):
            edge_ref[f, x : x + 1, :] = source[f % 3, x, 0:1, :]


def pack(chan_window, chan_dir, chan_local, part_row, elem_row, adj, fwd):
    coef = np.tile(time_filter().astype(np.float32)[:, None], (1, 128))
    hbm = pl.BlockSpec(memory_space=pl.ANY)
    return pl.pallas_call(
        pack_kernel,
        out_shape=[
            jax.ShapeDtypeStruct((NDEV * 8, 128), f32),
            jax.ShapeDtypeStruct((6, 8, 128), f32),
        ],
        in_specs=[hbm] * 9,
        scratch_shapes=[
            pltpu.VMEM((13 * 64, 256), f32),
            pltpu.VMEM((NSAMP, NCH), f32),
            pltpu.VMEM((3, NCH), f32),
            pltpu.VMEM((3, NCH), f32),
            pltpu.VMEM((1, NCH), i32),
            pltpu.VMEM((1, NCH), i32),
            pltpu.VMEM((NSAMP, 128), f32),
            pltpu.VMEM((256, 256), bf16),
            pltpu.VMEM((3, 8, 8, 128), f32),
            pltpu.VMEM((3, 8, 8, 128), f32),
            pltpu.SemaphoreType.DMA((9,)),
        ]
        + [pltpu.VMEM((13 * 64, PACK_CHUNK), bf16)] * PACK_UNROLL,
        compiler_params=pltpu.CompilerParams(vmem_limit_bytes=LIMIT),
        cost_estimate=pl.CostEstimate(
            flops=5 * 10**9, bytes_accessed=1500000, transcendentals=0
        ),
        name="pack",
    )(
        chan_window,
        chan_dir,
        chan_local,
        part_row,
        elem_row,
        jnp.asarray(coef),
        jnp.asarray(UPPER, bf16),
        adj,
        fwd,
    )


def select_matrix():
    lane = lax.broadcasted_iota(i32, (1, 640), 1)
    at = 4 * (lane & 31) + (lane >> 7)
    row = (lane >> 5) & 3
    parts = [one_hot(jnp.where(row == ey, at, 255).astype(f32), 128) for ey in range(EY)]
    return jnp.concatenate(parts, axis=0)


def element_kernel(
    adj_ref,
    fwd_ref,
    strike_ref,
    dip_ref,
    shear_ref,
    lame_ref,
    mu_ref,
    kappa_ref,
    table_ref,
    mu_out,
    kappa_out,
    force_out,
    n_ref,
    x_ref,
    u_ref,
    g_ref,
    t_ref,
):
    in_x = lax.axis_index("gx") < lax.axis_size("gx") - 1
    in_y = lax.axis_index("gy") < lax.axis_size("gy") - 1
    for f in range(6):
        source = adj_ref if f < 3 else fwd_ref
        for x in range(9):
            base = (f * 9 + x) * 24
            inside = in_y
            if x < 8:
                n_ref[base : base + 16, :] = source[f % 3, x]
            else:
                n_ref[base : base + 16, :] = jnp.where(in_x, strike_ref[f], 0.0)
                inside = in_x & in_y
            n_ref[base + 16 : base + 24, :] = jnp.zeros((8, 128), f32)
            n_ref[base + 16 : base + 17, :] = jnp.where(inside, dip_ref[f, x : x + 1, :], 0.0)
    for f in range(6):
        for ex in range(EX):
            for a in range(5):
                for ey in range(EY):
                    base = (f * 9 + 4 * ex + a) * 24 + 4 * ey
                    at = (f * 2 + ex) * 40 + a * 8
                    x_ref[at : at + 8, ey * 128 : (ey + 1) * 128] = n_ref[base : base + 8, :]
    whole = x_ref[...]
    top, rest = whole.astype(bf16), None
    rest = whole - top.astype(f32)
    mid = rest.astype(bf16)
    low = (rest - mid.astype(f32)).astype(bf16)
    select = select_matrix()
    opened = (dot(low, select) + dot(mid, select)) + dot(top, select)
    for block in range(12):
        for c in range(5):
            u_ref[c * 40 : (c + 1) * 40, block * 128 : (block + 1) * 128] = opened[
                block * 40 : (block + 1) * 40, c * 128 : (c + 1) * 128
            ]
    u_ref[200:208, :] = jnp.zeros((8, 1536), f32)
    top, low = split2(u_ref[...])
    both = dot(table_ref[0:768, 0:208], top)
    g_ref[...] = both[:384] + (both[384:] + dot(table_ref[0:384, 0:208], low))
    for ex in range(EX):
        lanes = slice(ex * 128, (ex + 1) * 128)
        shear = jnp.concatenate([shear_ref[ex, ey : ey + 1, :] for ey in range(EY)], axis=1)
        lame = jnp.concatenate([lame_ref[ex, ey : ey + 1, :] for ey in range(EY)], axis=1)
        bulk = lame + 2.0 / 3.0 * shear
        for tile in range(16):
            rows = slice(tile * 8, tile * 8 + 8)

            def grad(f, i, j):
                block = (f * 3 + i) * 2 + ex
                return g_ref[j * 128 + tile * 8 : j * 128 + tile * 8 + 8, block * 128 : (block + 1) * 128]

            strains = []
            for f in range(2):
                strain = {}
                for i in range(3):
                    strain[i, i] = grad(f, i, i)
                    for j in range(i):
                        strain[i, j] = 0.5 * (grad(f, i, j) + grad(f, j, i))
                        strain[j, i] = strain[i, j]
                strains.append(strain)
            adj, fwd = strains
            adj_trace = adj[0, 0] + adj[1, 1] + adj[2, 2]
            fwd_trace = fwd[0, 0] + fwd[1, 1] + fwd[2, 2]
            twice = 2.0 * shear
            pressure = lame * adj_trace
            for i in range(3):
                for j in range(3):
                    value = twice * adj[i, j]
                    if i == j:
                        value = value + pressure
                    block = i * 2 + ex
                    t_ref[j * 128 + tile * 8 : j * 128 + tile * 8 + 8, block * 128 : (block + 1) * 128] = value
            traces = adj_trace * fwd_trace
            product = (
                adj[0, 0] * fwd[0, 0] + adj[1, 1] * fwd[1, 1] + adj[2, 2] * fwd[2, 2]
            ) - traces * (1.0 / 3.0)
            product = product + 2.0 * (
                adj[1, 0] * fwd[1, 0] + adj[2, 0] * fwd[2, 0] + adj[2, 1] * fwd[2, 1]
            )
            count = 8 if tile < 15 else 5
            rows = slice(tile * 8, tile * 8 + count)
            mu_out[rows, lanes] = mu_ref[rows, lanes] + (time_step * twice * product)[:count]
            kappa_out[rows, lanes] = kappa_ref[rows, lanes] + (time_step * bulk * traces)[:count]
    top, low = split2(t_ref[...])
    both = dot(table_ref[768:1024, :], top)
    result = both[:128] + (both[128:] + dot(table_ref[768:896, :], low))
    for i in range(3):
        lanes = slice(i * 256, (i + 1) * 256)
        force_out[i * 120 : (i + 1) * 120, :] = result[:120, lanes]
        force_out[360 + i * 5 : 365 + i * 5, :] = result[120:125, lanes]
    force_out[375:384, :] = jnp.zeros((9, ELEMS), f32)


def element_terms(adj, fwd, strike, dip, shear, lame, mu, kappa):
    grad = np.concatenate(halves(GRAD), axis=0)
    table = np.zeros((1024, 384), grad.dtype)
    table[:768, :208] = grad
    table[768:] = np.concatenate(halves(DIV), axis=0)
    return pl.pallas_call(
        element_kernel,
        out_shape=[
            jax.ShapeDtypeStruct((125, ELEMS), f32),
            jax.ShapeDtypeStruct((125, ELEMS), f32),
            jax.ShapeDtypeStruct((384, ELEMS), f32),
        ],
        scratch_shapes=[
            pltpu.VMEM((6 * 9 * 24, 128), f32),
            pltpu.VMEM((480, 512), f32),
            pltpu.VMEM((208, 1536), f32),
            pltpu.VMEM((384, 1536), f32),
            pltpu.VMEM((384, 768), f32),
        ],
        compiler_params=pltpu.CompilerParams(vmem_limit_bytes=LOW_LIMIT),
        cost_estimate=pl.CostEstimate(
            flops=5 * 10**9, bytes_accessed=5000000, transcendentals=0
        ),
        name="element_terms",
    )(adj, fwd, strike, dip, shear, lame, mu, kappa, jnp.asarray(table))


GROUP = 8
SPREAD_UNROLL = 8


def source_kernel(
    inc_ref,
    div_ref,
    table_ref,
    main_out,
    dip_out,
    strike_out,
    corner_out,
    acc_ref,
    z_ref,
    f_ref,
    *parts_refs,
):
    turns = 128 // GROUP // SPREAD_UNROLL
    acc_ref[...] = jnp.zeros_like(acc_ref)

    def basis(points):
        gaps = [points - float(np.float32(nodes[m])) for m in range(5)]
        result = []
        for p in range(5):
            scale = 1.0
            value = None
            for m in range(5):
                if m != p:
                    scale = scale / (nodes[p] - nodes[m])
                    value = gaps[m] if value is None else value * gaps[m]
            result.append(value * float(scale))
        return result

    def spread(at, gx_ref, yz_ref, a_ref, b_ref):
        for sub in range(GROUP // 8):
            base = pl.multiple_of(at * (GROUP * 8) + sub * 64, 64)
            values = [inc_ref[pl.ds(base + v, 8, stride=8), :] for v in range(7)]
            lx, ly, lz = basis(values[3]), basis(values[4]), basis(values[5])
            for i in range(3):
                for a in range(5):
                    gx_ref[pl.ds(sub * 128 + i * 5 + a, 8, stride=16), :] = values[i] * lx[a]
            gx_ref[pl.ds(sub * 128 + 15, 8, stride=16), :] = jnp.zeros((8, 128), f32)
            for b in range(5):
                for c in range(5):
                    yz_ref[pl.ds(sub * 256 + b * 5 + c, 8, stride=32), :] = ly[b] * lz[c]
            index = values[6]
            for k in range(8):
                s = sub * 8 + k
                lanes = slice(s * 128, (s + 1) * 128)
                b_ref[:, lanes] = one_hot(index[k : k + 1, :], ELEMS)
                yz = yz_ref[s * 32 : s * 32 + 24, :]
                last = yz_ref[s * 32 + 24 : s * 32 + 25, :]
                for pair in range(8):
                    row = s * 16 + 2 * pair
                    parts = [gx_ref[row : row + 1, :] * yz]
                    if pair < 7:
                        parts += [gx_ref[row + 1 : row + 2, :] * yz]
                    else:
                        parts += [gx_ref[s * 16 : s * 16 + 16, :] * last, jnp.zeros((8, 128), f32)]
                    top, low = split2(jnp.concatenate(parts, axis=0))
                    a_ref[pair * 48 : pair * 48 + 48, lanes] = top
                    a_ref[384 + pair * 48 : 384 + pair * 48 + 48, lanes] = low

    def gather(gx_ref, yz_ref, a_ref, b_ref):
        acc_ref[...] += dot_nt(a_ref[...], b_ref[...])

    sets = [parts_refs[4 * k : 4 * k + 4] for k in range(SPREAD_UNROLL)]

    def step(at, carry):
        for k in range(SPREAD_UNROLL):
            spread(at * SPREAD_UNROLL + k, *sets[k])
            gather(*sets[k])
        return carry

    lax.fori_loop(0, turns, step, 0)
    total = acc_ref[0:384, :] + acc_ref[384:768, :] - div_ref[...]
    top, low = split2(total)
    place = table_ref[0:608, 0:384]
    placed = dot(place, top) + dot(place, low)
    for i in range(3):
        for c in range(5):
            at = i * 200 + c * 40
            block = placed[at : at + 40, :]
            for ex in range(EX):
                to = (i * 2 + ex) * 40
                z_ref[to : to + 40, c * 128 : (c + 1) * 128] = block[:, ex * 128 : (ex + 1) * 128]
    top, low = split2(z_ref[...])
    back = table_ref[608:1248, :]
    nodal = dot(top, back) + dot(low, back)
    f_ref[...] = jnp.zeros_like(f_ref)
    for i in range(3):
        for ex in range(EX):
            for a in range(5):
                at = (i * 2 + ex) * 40 + a * 8
                for ey in range(EY):
                    to = (i * 9 + 4 * ex + a) * 24 + 4 * ey
                    f_ref[to : to + 8, :] += nodal[at : at + 8, ey * 128 : (ey + 1) * 128]
    for i in range(3):
        for x in range(9):
            at = (i * 9 + x) * 24
            if x < 8:
                main_out[i, x] = f_ref[at : at + 16, :]
                dip_out[i, x : x + 1, :] = f_ref[at + 16 : at + 17, :]
            else:
                strike_out[i] = f_ref[at : at + 16, :]
                corner_out[i, 0:24, :] = f_ref[at : at + 24, :]
                corner_out[i, 24:32, :] = jnp.zeros((8, 128), f32)
                dip_out[i, 8:24, :] = jnp.zeros((16, 128), f32)


def source_forces(incoming, divergence):
    table = np.zeros((1248, 512), np.float32)
    table[:608, :384] = PLACE
    table[608:] = SELECT.T
    return pl.pallas_call(
        source_kernel,
        out_shape=[
            jax.ShapeDtypeStruct((3, 8, 16, 128), f32),
            jax.ShapeDtypeStruct((3, 24, 128), f32),
            jax.ShapeDtypeStruct((3, 16, 128), f32),
            jax.ShapeDtypeStruct((3, 32, 128), f32),
        ],
        scratch_shapes=[
            pltpu.VMEM((768, 256), f32),
            pltpu.VMEM((240, 640), f32),
            pltpu.VMEM((3 * 9 * 24, 128), f32),
        ]
        + [
            pltpu.VMEM((GROUP * 16, 128), f32),
            pltpu.VMEM((GROUP * 32, 128), f32),
            pltpu.VMEM((768, GROUP * 128), bf16),
            pltpu.VMEM((256, GROUP * 128), bf16),
        ]
        * SPREAD_UNROLL,
        compiler_params=pltpu.CompilerParams(vmem_limit_bytes=32 * 1024 * 1024),
        name="source_forces",
    )(incoming, divergence, jnp.asarray(table, bf16))


def update_kernel(
    disp_ref, veloc_ref, mass_ref, force_ref, dip_ref, strike_ref, corner_ref, disp_out, veloc_out, f_ref
):
    in_x = lax.axis_index("gx") > 0
    in_y = lax.axis_index("gy") > 0
    f_ref[...] = force_ref[...]
    for i in range(3):
        for x in range(8):
            f_ref[i, x, 0:1, :] += jnp.where(in_y, dip_ref[i, x : x + 1, :], 0.0)
        f_ref[i, 0] += jnp.where(in_x, strike_ref[i], 0.0)
        f_ref[i, 0, 0:1, :] += jnp.where(in_x & in_y, corner_ref[i, 16:17, :], 0.0)
    for i in range(3):
        veloc = veloc_ref[i] + time_step * (mass_ref[...] * f_ref[i])
        veloc_out[i] = veloc
        disp_out[i] = disp_ref[i] + time_step * veloc


def update(disp, veloc, mass, force, dip, strike, corner):
    shape = jax.ShapeDtypeStruct((3, 8, 16, 128), f32)
    return pl.pallas_call(
        update_kernel,
        out_shape=[shape, shape],
        scratch_shapes=[pltpu.VMEM((3, 8, 16, 128), f32)],
        compiler_params=pltpu.CompilerParams(vmem_limit_bytes=8 * 1024 * 1024),
        name="update",
    )(disp, veloc, mass, force, dip, strike, corner)


def local(
    adj_disp,
    adj_veloc,
    fwd_disp,
    inv_mass,
    shear_mod,
    lame_mod,
    kernel_mu,
    kernel_kappa,
    chan_window,
    chan_dir,
    chan_local,
    chan_part,
    chan_elem,
):
    first = jnp.concatenate([adj_disp[:, 0], fwd_disp[:, 0]], axis=0)
    strike = shifted(first, -1, 0)
    outgoing, edge = pack(
        chan_window,
        chan_dir,
        chan_local,
        chan_part.reshape(1, NCH),
        chan_elem.reshape(1, NCH),
        adj_disp,
        fwd_disp,
    )
    incoming = lax.all_to_all(
        outgoing.reshape(NDEV, 8, 128), ("gx", "gy"), split_axis=0, concat_axis=0, tiled=True
    )
    dip = shifted(jnp.concatenate([edge, strike[:, 0:1]], axis=1), 0, -1)
    mu_new, kappa_new, divergence = element_terms(
        adj_disp, fwd_disp, strike, dip, shear_mod, lame_mod, kernel_mu, kernel_kappa
    )
    force, dip_force, strike_force, corner_force = source_forces(
        incoming.reshape(NDEV * 8, 128), divergence
    )
    disp_new, veloc_new = update(
        adj_disp,
        adj_veloc,
        inv_mass,
        force,
        shifted(dip_force, 0, 1),
        shifted(strike_force, 1, 0),
        shifted(corner_force, 1, 1),
    )
    return (disp_new, veloc_new, mu_new, kappa_new)


def solution(mesh):
    return jax.shard_map(
        local,
        mesh=mesh,
        in_specs=(
            P(None, "gx", "gy", None),
            P(None, "gx", "gy", None),
            P(None, "gx", "gy", None),
            P("gx", "gy", None),
            P("gx", "gy", None),
            P("gx", "gy", None),
            P(None, ("gx", "gy")),
            P(None, ("gx", "gy")),
            P(None, ("gx", "gy")),
            P(None, ("gx", "gy")),
            P(None, ("gx", "gy")),
            P(("gx", "gy"), None),
            P(("gx", "gy")),
        ),
        out_specs=(
            P(None, "gx", "gy", None),
            P(None, "gx", "gy", None),
            P(None, ("gx", "gy")),
            P(None, ("gx", "gy")),
        ),
        check_vma=False,
    )
```

```python
import jax
import jax.numpy as jnp
import numpy as np
from jax import lax
from jax.experimental import pallas as pl
from jax.experimental.pallas import tpu as pltpu
from jax.sharding import PartitionSpec as P

NSAMP = 16
time_step = 0.05
f32, bf16, i32 = jnp.float32, jnp.bfloat16, jnp.int32

EX, EY, EZ = 2, 4, 32
NCH = 8192
NDEV = 128
CAP = 128
ELEMS = EX * EY * EZ
LIMIT = 56 * 1024 * 1024
LOW_LIMIT = 24 * 1024 * 1024


def gll_tables():
    gll_nodes = np.array([-1.0, -np.sqrt(3.0 / 7.0), 0.0, np.sqrt(3.0 / 7.0), 1.0])
    gll_weights = np.array([0.1, 49.0 / 90.0, 32.0 / 45.0, 49.0 / 90.0, 0.1])
    derivative = np.zeros((5, 5))
    for a in range(5):
        for p in range(5):
            summed = 0.0
            for m in range(5):
                if m != p:
                    factor = 1.0 / (gll_nodes[p] - gll_nodes[m])
                    for k in range(5):
                        if k != p and k != m:
                            factor = (
                                factor
                                * (gll_nodes[a] - gll_nodes[k])
                                / (gll_nodes[p] - gll_nodes[k])
                            )
                    summed = summed + factor
            derivative[a, p] = summed
    return (gll_nodes, gll_weights, derivative)


def time_filter():
    offsets = np.arange(NSAMP) - (NSAMP - 1) / 2.0
    cardinal = np.sin(np.pi * offsets) / (np.pi * offsets)
    values = cardinal * (0.5 + 0.5 * np.cos(np.pi * offsets / (NSAMP / 2.0)))
    return values / np.sum(values)


nodes, weights, deriv = gll_tables()


def halves(matrix):
    matrix = np.asarray(matrix, np.float32)
    top = matrix.astype(jnp.bfloat16)
    low = (matrix - top.astype(np.float32)).astype(jnp.bfloat16)
    return top, low


def padded_row(c, a, b):
    return c * 40 + a * 8 + b


def build_tables():
    select = np.zeros((EY * 128, 5 * 128), np.float32)
    for ey in range(EY):
        for c in range(5):
            for ez in range(EZ):
                if 4 * ez + c < 128:
                    select[ey * 128 + 4 * ez + c, c * 128 + ey * 32 + ez] = 1.0
    grad = np.zeros((384, 208))
    div = np.zeros((128, 384))
    for a in range(5):
        for b in range(5):
            for c in range(5):
                row = 25 * a + 5 * b + c
                for p in range(5):
                    grad[row, padded_row(c, p, b)] += deriv[a, p]
                    grad[128 + row, padded_row(c, a, p)] += deriv[b, p]
                    grad[256 + row, padded_row(p, a, b)] += deriv[c, p]
                    bc = 5 * b + c
                    out = a * 24 + bc if bc < 24 else 120 + a
                    div[out, 25 * p + 5 * b + c] += (
                        deriv[p, a] * weights[p] * weights[b] * weights[c]
                    )
                    div[out, 128 + 25 * a + 5 * p + c] += (
                        deriv[p, b] * weights[a] * weights[p] * weights[c]
                    )
                    div[out, 256 + 25 * a + 5 * b + p] += (
                        deriv[p, c] * weights[a] * weights[b] * weights[p]
                    )
    place = np.zeros((608, 384), np.float32)
    for i in range(3):
        for a in range(5):
            for b in range(5):
                for c in range(5):
                    bc = 5 * b + c
                    at = (i * 5 + a) * 24 + bc if bc < 24 else 360 + i * 5 + a
                    place[i * 200 + padded_row(c, a, b), at] = 1.0
    upper = np.asarray(np.arange(256)[:, None] <= np.arange(256)[None, :], np.float32)
    return select, grad, div, place, upper


SELECT, GRAD, DIV, PLACE, UPPER = build_tables()


def shifted(x, step_x, step_y):
    size_x, size_y = lax.axis_size("gx"), lax.axis_size("gy")
    if step_y == 0:
        return lax.ppermute(x, "gx", [(i, (i + step_x) % size_x) for i in range(size_x)])
    if step_x == 0:
        return lax.ppermute(x, "gy", [(i, (i + step_y) % size_y) for i in range(size_y)])
    pairs = [
        (i * size_y + j, (i + step_x) % size_x * size_y + (j + step_y) % size_y)
        for i in range(size_x)
        for j in range(size_y)
    ]
    return lax.ppermute(x, ("gx", "gy"), pairs)


def dot(x, y):
    return jnp.dot(x, y, preferred_element_type=f32)


def dot_nt(x, y):
    return lax.dot_general(x, y, (((1,), (1,)), ((), ())), preferred_element_type=f32)


def split2(x):
    top = x.astype(bf16)
    return top, (x - top.astype(f32)).astype(bf16)


def low_row(row, rows):
    tile = jnp.broadcast_to(row, (16, row.shape[1])).astype(bf16)
    return jnp.concatenate([tile] * (rows // 16), axis=0)


def one_hot(row, rows):
    numbers = lax.broadcasted_iota(i32, (rows, row.shape[1]), 0).astype(f32).astype(bf16)
    return jnp.where(numbers == low_row(row, rows), jnp.ones((), bf16), jnp.zeros((), bf16))


PACK_CHUNK = 2048
PACK_UNROLL = 2


def pack_kernel(
    win_hbm,
    dir_hbm,
    loc_hbm,
    part_hbm,
    elem_hbm,
    coef_hbm,
    upper_hbm,
    adj_hbm,
    fwd_hbm,
    out_ref,
    edge_ref,
    acc_ref,
    win_ref,
    dir_ref,
    loc_ref,
    part_ref,
    elem_ref,
    coef_ref,
    upper_ref,
    adj_ref,
    fwd_ref,
    sems,
    *a_refs,
):
    edge = pl.ds(0, 8)
    pairs = [
        (upper_hbm, upper_ref),
        (part_hbm, part_ref),
        (win_hbm, win_ref),
        (coef_hbm, coef_ref),
        (dir_hbm, dir_ref),
        (loc_hbm, loc_ref),
        (elem_hbm, elem_ref),
        (adj_hbm.at[:, :, edge, :], adj_ref),
        (fwd_hbm.at[:, :, edge, :], fwd_ref),
    ]
    copies = [pltpu.make_async_copy(a, b, sems.at[k]) for k, (a, b) in enumerate(pairs)]
    for copy in copies:
        copy.start()
    acc_ref[...] = jnp.zeros_like(acc_ref)
    for copy in copies[:7]:
        copy.wait()
    upper = upper_ref[...]
    coef = coef_ref[:, 0:1]

    def fill(at, base, a_ref):
        blocks = PACK_CHUNK // 256
        targets, same = [], []
        for block in range(blocks):
            span = pl.ds(pl.multiple_of(at * PACK_CHUNK + block * 256, 256), 256)
            targets.append(part_ref[:, span])
            same.append(lax.broadcasted_iota(i32, (NDEV, 256), 0) == targets[block])
        hits = jnp.concatenate([jnp.where(hit, 1.0, 0.0).astype(bf16) for hit in same], axis=0)
        running = dot(hits, upper)
        keys = []
        for block in range(blocks):
            upto = running[block * NDEV : (block + 1) * NDEV, :]
            rank = jnp.sum(jnp.where(same[block], upto + base, 0.0), axis=0, keepdims=True)
            keys.append(rank + ((targets[block] >> 6) * CAP - 1).astype(f32))
            base = base + upto[:, 255:256]
        key = jnp.concatenate(keys, axis=1)
        span = pl.ds(pl.multiple_of(at * PACK_CHUNK, PACK_CHUNK), PACK_CHUNK)
        strength = jnp.sum(win_ref[:, span] * coef, axis=0, keepdims=True)
        force = strength * dir_ref[:, span]
        where_at = loc_ref[:, span]
        force_low = force - force.astype(bf16).astype(f32)
        where_low = where_at - where_at.astype(bf16).astype(f32)
        elem = elem_ref[:, span].astype(f32)
        rows = [force[k : k + 1] for k in range(3)] + [where_at[k : k + 1] for k in range(3)]
        rows += [force_low[k : k + 1] for k in range(3)] + [where_low[k : k + 1] for k in range(3)]
        rows += [elem]
        mask = one_hot((part_ref[:, span] & 63).astype(f32), 64)
        for k, row in enumerate(rows):
            a_ref[k * 64 : (k + 1) * 64, :] = mask * low_row(row, 64)
        acc_ref[...] += dot_nt(a_ref[...], one_hot(key, 256))
        return base

    def step(at, base):
        for k in range(PACK_UNROLL):
            base = fill(at * PACK_UNROLL + k, base, a_refs[k])
        return base

    lax.fori_loop(0, NCH // PACK_CHUNK // PACK_UNROLL, step, jnp.zeros((NDEV, 1), f32))
    for half in range(2):
        lanes = slice(half * 128, (half + 1) * 128)
        for v in range(6):
            out_ref[pl.ds(half * 512 + v, 64, stride=8), :] = (
                acc_ref[v * 64 : (v + 1) * 64, lanes] + acc_ref[(6 + v) * 64 : (7 + v) * 64, lanes]
            )
        out_ref[pl.ds(half * 512 + 6, 64, stride=8), :] = acc_ref[12 * 64 : 13 * 64, lanes]
        out_ref[pl.ds(half * 512 + 7, 64, stride=8), :] = jnp.zeros((64, 128), f32)
    for copy in copies[7:]:
        copy.wait()
    for f in range(6):
        source = adj_ref if f < 3 else fwd_ref
        for x in range(8):
            edge_ref[f, x : x + 1, :] = source[f % 3, x, 0:1, :]


def pack(chan_window, chan_dir, chan_local, part_row, elem_row, adj, fwd):
    coef = np.tile(time_filter().astype(np.float32)[:, None], (1, 128))
    hbm = pl.BlockSpec(memory_space=pl.ANY)
    return pl.pallas_call(
        pack_kernel,
        out_shape=[
            jax.ShapeDtypeStruct((NDEV * 8, 128), f32),
            jax.ShapeDtypeStruct((6, 8, 128), f32),
        ],
        in_specs=[hbm] * 9,
        scratch_shapes=[
            pltpu.VMEM((13 * 64, 256), f32),
            pltpu.VMEM((NSAMP, NCH), f32),
            pltpu.VMEM((3, NCH), f32),
            pltpu.VMEM((3, NCH), f32),
            pltpu.VMEM((1, NCH), i32),
            pltpu.VMEM((1, NCH), i32),
            pltpu.VMEM((NSAMP, 128), f32),
            pltpu.VMEM((256, 256), bf16),
            pltpu.VMEM((3, 8, 8, 128), f32),
            pltpu.VMEM((3, 8, 8, 128), f32),
            pltpu.SemaphoreType.DMA((9,)),
        ]
        + [pltpu.VMEM((13 * 64, PACK_CHUNK), bf16)] * PACK_UNROLL,
        compiler_params=pltpu.CompilerParams(vmem_limit_bytes=LIMIT),
        cost_estimate=pl.CostEstimate(
            flops=5 * 10**9, bytes_accessed=1500000, transcendentals=0
        ),
        name="pack",
    )(
        chan_window,
        chan_dir,
        chan_local,
        part_row,
        elem_row,
        jnp.asarray(coef),
        jnp.asarray(UPPER, bf16),
        adj,
        fwd,
    )


def select_matrix():
    lane = lax.broadcasted_iota(i32, (1, 640), 1)
    at = 4 * (lane & 31) + (lane >> 7)
    row = (lane >> 5) & 3
    parts = [one_hot(jnp.where(row == ey, at, 255).astype(f32), 128) for ey in range(EY)]
    return jnp.concatenate(parts, axis=0)


def element_kernel(
    adj_ref,
    fwd_ref,
    strike_ref,
    dip_ref,
    shear_ref,
    lame_ref,
    mu_ref,
    kappa_ref,
    table_ref,
    mu_out,
    kappa_out,
    force_out,
    n_ref,
    x_ref,
    u_ref,
    g_ref,
    t_ref,
):
    in_x = lax.axis_index("gx") < lax.axis_size("gx") - 1
    in_y = lax.axis_index("gy") < lax.axis_size("gy") - 1
    for f in range(6):
        source = adj_ref if f < 3 else fwd_ref
        for x in range(9):
            base = (f * 9 + x) * 24
            inside = in_y
            if x < 8:
                n_ref[base : base + 16, :] = source[f % 3, x]
            else:
                n_ref[base : base + 16, :] = jnp.where(in_x, strike_ref[f], 0.0)
                inside = in_x & in_y
            n_ref[base + 16 : base + 24, :] = jnp.zeros((8, 128), f32)
            n_ref[base + 16 : base + 17, :] = jnp.where(inside, dip_ref[f, x : x + 1, :], 0.0)
    for f in range(6):
        for ex in range(EX):
            for a in range(5):
                for ey in range(EY):
                    base = (f * 9 + 4 * ex + a) * 24 + 4 * ey
                    at = (f * 2 + ex) * 40 + a * 8
                    x_ref[at : at + 8, ey * 128 : (ey + 1) * 128] = n_ref[base : base + 8, :]
    whole = x_ref[...]
    top, rest = whole.astype(bf16), None
    rest = whole - top.astype(f32)
    mid = rest.astype(bf16)
    low = (rest - mid.astype(f32)).astype(bf16)
    select = select_matrix()
    opened = (dot(low, select) + dot(mid, select)) + dot(top, select)
    for block in range(12):
        for c in range(5):
            u_ref[c * 40 : (c + 1) * 40, block * 128 : (block + 1) * 128] = opened[
                block * 40 : (block + 1) * 40, c * 128 : (c + 1) * 128
            ]
    u_ref[200:208, :] = jnp.zeros((8, 1536), f32)
    top, low = split2(u_ref[...])
    both = dot(table_ref[:, 0:208], top)
    g_ref[...] = both[:384] + (both[384:] + dot(table_ref[0:384, 0:208], low))
    for ex in range(EX):
        lanes = slice(ex * 128, (ex + 1) * 128)
        shear = jnp.concatenate([shear_ref[ex, ey : ey + 1, :] for ey in range(EY)], axis=1)
        lame = jnp.concatenate([lame_ref[ex, ey : ey + 1, :] for ey in range(EY)], axis=1)
        bulk = lame + 2.0 / 3.0 * shear
        for tile in range(16):
            rows = slice(tile * 8, tile * 8 + 8)

            def grad(f, i, j):
                block = (f * 3 + i) * 2 + ex
                return g_ref[j * 128 + tile * 8 : j * 128 + tile * 8 + 8, block * 128 : (block + 1) * 128]

            strains = []
            for f in range(2):
                strain = {}
                for i in range(3):
                    strain[i, i] = grad(f, i, i)
                    for j in range(i):
                        strain[i, j] = 0.5 * (grad(f, i, j) + grad(f, j, i))
                        strain[j, i] = strain[i, j]
                strains.append(strain)
            adj, fwd = strains
            adj_trace = adj[0, 0] + adj[1, 1] + adj[2, 2]
            fwd_trace = fwd[0, 0] + fwd[1, 1] + fwd[2, 2]
            twice = 2.0 * shear
            pressure = lame * adj_trace
            for i in range(3):
                for j in range(3):
                    value = twice * adj[i, j]
                    if i == j:
                        value = value + pressure
                    block = i * 2 + ex
                    t_ref[j * 128 + tile * 8 : j * 128 + tile * 8 + 8, block * 128 : (block + 1) * 128] = value
            traces = adj_trace * fwd_trace
            product = (
                adj[0, 0] * fwd[0, 0] + adj[1, 1] * fwd[1, 1] + adj[2, 2] * fwd[2, 2]
            ) - traces * (1.0 / 3.0)
            product = product + 2.0 * (
                adj[1, 0] * fwd[1, 0] + adj[2, 0] * fwd[2, 0] + adj[2, 1] * fwd[2, 1]
            )
            count = 8 if tile < 15 else 5
            rows = slice(tile * 8, tile * 8 + count)
            mu_out[rows, lanes] = mu_ref[rows, lanes] + (time_step * twice * product)[:count]
            kappa_out[rows, lanes] = kappa_ref[rows, lanes] + (time_step * bulk * traces)[:count]
    top, low = split2(t_ref[...])
    result = jnp.zeros((128, 768), f32)
    for j in range(3):
        rows = slice(j * 128, (j + 1) * 128)
        both = dot(table_ref[j * 256 : (j + 1) * 256, 256:384], top[rows])
        rest = dot(table_ref[j * 256 : j * 256 + 128, 256:384], low[rows])
        result = result + (both[:128] + (both[128:] + rest))
    for i in range(3):
        lanes = slice(i * 256, (i + 1) * 256)
        force_out[i * 120 : (i + 1) * 120, :] = result[:120, lanes]
        force_out[360 + i * 5 : 365 + i * 5, :] = result[120:125, lanes]
    force_out[375:384, :] = jnp.zeros((9, ELEMS), f32)


def element_terms(adj, fwd, strike, dip, shear, lame, mu, kappa):
    grad = np.concatenate(halves(GRAD), axis=0)
    table = np.zeros((768, 384), grad.dtype)
    table[:, :208] = grad
    for j in range(3):
        block = DIV[:, j * 128 : (j + 1) * 128]
        table[j * 256 : (j + 1) * 256, 256:] = np.concatenate(halves(block), axis=0)
    return pl.pallas_call(
        element_kernel,
        out_shape=[
            jax.ShapeDtypeStruct((125, ELEMS), f32),
            jax.ShapeDtypeStruct((125, ELEMS), f32),
            jax.ShapeDtypeStruct((384, ELEMS), f32),
        ],
        scratch_shapes=[
            pltpu.VMEM((6 * 9 * 24, 128), f32),
            pltpu.VMEM((480, 512), f32),
            pltpu.VMEM((208, 1536), f32),
            pltpu.VMEM((384, 1536), f32),
            pltpu.VMEM((384, 768), f32),
        ],
        compiler_params=pltpu.CompilerParams(vmem_limit_bytes=LOW_LIMIT),
        cost_estimate=pl.CostEstimate(
            flops=5 * 10**9, bytes_accessed=5000000, transcendentals=0
        ),
        name="element_terms",
    )(adj, fwd, strike, dip, shear, lame, mu, kappa, jnp.asarray(table))


GROUP = 8
SPREAD_UNROLL = 8


def source_kernel(
    inc_ref,
    div_ref,
    table_ref,
    main_out,
    dip_out,
    strike_out,
    corner_out,
    acc_ref,
    z_ref,
    f_ref,
    *parts_refs,
):
    turns = 128 // GROUP // SPREAD_UNROLL
    acc_ref[...] = jnp.zeros_like(acc_ref)

    def basis(points):
        gaps = [points - float(np.float32(nodes[m])) for m in range(5)]
        result = []
        for p in range(5):
            scale = 1.0
            value = None
            for m in range(5):
                if m != p:
                    scale = scale / (nodes[p] - nodes[m])
                    value = gaps[m] if value is None else value * gaps[m]
            result.append(value * float(scale))
        return result

    def spread(at, gx_ref, yz_ref, a_ref, b_ref):
        for sub in range(GROUP // 8):
            base = pl.multiple_of(at * (GROUP * 8) + sub * 64, 64)
            values = [inc_ref[pl.ds(base + v, 8, stride=8), :] for v in range(7)]
            lx, ly, lz = basis(values[3]), basis(values[4]), basis(values[5])
            for i in range(3):
                for a in range(5):
                    gx_ref[pl.ds(sub * 128 + i * 5 + a, 8, stride=16), :] = values[i] * lx[a]
            gx_ref[pl.ds(sub * 128 + 15, 8, stride=16), :] = jnp.zeros((8, 128), f32)
            for b in range(5):
                for c in range(5):
                    yz_ref[pl.ds(sub * 256 + b * 5 + c, 8, stride=32), :] = ly[b] * lz[c]
            index = values[6]
            for k in range(8):
                s = sub * 8 + k
                lanes = slice(s * 128, (s + 1) * 128)
                b_ref[:, lanes] = one_hot(index[k : k + 1, :], ELEMS)
                yz = yz_ref[s * 32 : s * 32 + 24, :]
                last = yz_ref[s * 32 + 24 : s * 32 + 25, :]
                for pair in range(8):
                    row = s * 16 + 2 * pair
                    parts = [gx_ref[row : row + 1, :] * yz]
                    if pair < 7:
                        parts += [gx_ref[row + 1 : row + 2, :] * yz]
                    else:
                        parts += [gx_ref[s * 16 : s * 16 + 16, :] * last, jnp.zeros((8, 128), f32)]
                    top, low = split2(jnp.concatenate(parts, axis=0))
                    a_ref[pair * 48 : pair * 48 + 48, lanes] = top
                    a_ref[384 + pair * 48 : 384 + pair * 48 + 48, lanes] = low

    def gather(gx_ref, yz_ref, a_ref, b_ref):
        acc_ref[...] += dot_nt(a_ref[...], b_ref[...])

    sets = [parts_refs[4 * k : 4 * k + 4] for k in range(SPREAD_UNROLL)]

    def step(at, carry):
        for k in range(SPREAD_UNROLL):
            spread(at * SPREAD_UNROLL + k, *sets[k])
            gather(*sets[k])
        return carry

    lax.fori_loop(0, turns, step, 0)
    total = acc_ref[0:384, :] + acc_ref[384:768, :] - div_ref[...]
    top, low = split2(total)
    place = table_ref[0:608, 0:384]
    placed = dot(place, top) + dot(place, low)
    for i in range(3):
        for c in range(5):
            at = i * 200 + c * 40
            block = placed[at : at + 40, :]
            for ex in range(EX):
                to = (i * 2 + ex) * 40
                z_ref[to : to + 40, c * 128 : (c + 1) * 128] = block[:, ex * 128 : (ex + 1) * 128]
    top, low = split2(z_ref[...])
    back = table_ref[608:1248, :]
    nodal = dot(top, back) + dot(low, back)
    f_ref[...] = jnp.zeros_like(f_ref)
    for i in range(3):
        for ex in range(EX):
            for a in range(5):
                at = (i * 2 + ex) * 40 + a * 8
                for ey in range(EY):
                    to = (i * 9 + 4 * ex + a) * 24 + 4 * ey
                    f_ref[to : to + 8, :] += nodal[at : at + 8, ey * 128 : (ey + 1) * 128]
    for i in range(3):
        for x in range(9):
            at = (i * 9 + x) * 24
            if x < 8:
                main_out[i, x] = f_ref[at : at + 16, :]
                dip_out[i, x : x + 1, :] = f_ref[at + 16 : at + 17, :]
            else:
                strike_out[i] = f_ref[at : at + 16, :]
                corner_out[i, 0:24, :] = f_ref[at : at + 24, :]
                corner_out[i, 24:32, :] = jnp.zeros((8, 128), f32)
                dip_out[i, 8:24, :] = jnp.zeros((16, 128), f32)


def source_forces(incoming, divergence):
    table = np.zeros((1248, 512), np.float32)
    table[:608, :384] = PLACE
    table[608:] = SELECT.T
    return pl.pallas_call(
        source_kernel,
        out_shape=[
            jax.ShapeDtypeStruct((3, 8, 16, 128), f32),
            jax.ShapeDtypeStruct((3, 24, 128), f32),
            jax.ShapeDtypeStruct((3, 16, 128), f32),
            jax.ShapeDtypeStruct((3, 32, 128), f32),
        ],
        scratch_shapes=[
            pltpu.VMEM((768, 256), f32),
            pltpu.VMEM((240, 640), f32),
            pltpu.VMEM((3 * 9 * 24, 128), f32),
        ]
        + [
            pltpu.VMEM((GROUP * 16, 128), f32),
            pltpu.VMEM((GROUP * 32, 128), f32),
            pltpu.VMEM((768, GROUP * 128), bf16),
            pltpu.VMEM((256, GROUP * 128), bf16),
        ]
        * SPREAD_UNROLL,
        compiler_params=pltpu.CompilerParams(vmem_limit_bytes=32 * 1024 * 1024),
        name="source_forces",
    )(incoming, divergence, jnp.asarray(table, bf16))


def update_kernel(
    disp_ref, veloc_ref, mass_ref, force_ref, dip_ref, strike_ref, corner_ref, disp_out, veloc_out, f_ref
):
    in_x = lax.axis_index("gx") > 0
    in_y = lax.axis_index("gy") > 0
    f_ref[...] = force_ref[...]
    for i in range(3):
        for x in range(8):
            f_ref[i, x, 0:1, :] += jnp.where(in_y, dip_ref[i, x : x + 1, :], 0.0)
        f_ref[i, 0] += jnp.where(in_x, strike_ref[i], 0.0)
        f_ref[i, 0, 0:1, :] += jnp.where(in_x & in_y, corner_ref[i, 16:17, :], 0.0)
    for i in range(3):
        veloc = veloc_ref[i] + time_step * (mass_ref[...] * f_ref[i])
        veloc_out[i] = veloc
        disp_out[i] = disp_ref[i] + time_step * veloc


def update(disp, veloc, mass, force, dip, strike, corner):
    shape = jax.ShapeDtypeStruct((3, 8, 16, 128), f32)
    return pl.pallas_call(
        update_kernel,
        out_shape=[shape, shape],
        scratch_shapes=[pltpu.VMEM((3, 8, 16, 128), f32)],
        compiler_params=pltpu.CompilerParams(vmem_limit_bytes=8 * 1024 * 1024),
        name="update",
    )(disp, veloc, mass, force, dip, strike, corner)


def local(
    adj_disp,
    adj_veloc,
    fwd_disp,
    inv_mass,
    shear_mod,
    lame_mod,
    kernel_mu,
    kernel_kappa,
    chan_window,
    chan_dir,
    chan_local,
    chan_part,
    chan_elem,
):
    first = jnp.concatenate([adj_disp[:, 0], fwd_disp[:, 0]], axis=0)
    strike = shifted(first, -1, 0)
    outgoing, edge = pack(
        chan_window,
        chan_dir,
        chan_local,
        chan_part.reshape(1, NCH),
        chan_elem.reshape(1, NCH),
        adj_disp,
        fwd_disp,
    )
    incoming = lax.all_to_all(
        outgoing.reshape(NDEV, 8, 128), ("gx", "gy"), split_axis=0, concat_axis=0, tiled=True
    )
    dip = shifted(jnp.concatenate([edge, strike[:, 0:1]], axis=1), 0, -1)
    mu_new, kappa_new, divergence = element_terms(
        adj_disp, fwd_disp, strike, dip, shear_mod, lame_mod, kernel_mu, kernel_kappa
    )
    force, dip_force, strike_force, corner_force = source_forces(
        incoming.reshape(NDEV * 8, 128), divergence
    )
    disp_new, veloc_new = update(
        adj_disp,
        adj_veloc,
        inv_mass,
        force,
        shifted(dip_force, 0, 1),
        shifted(strike_force, 1, 0),
        shifted(corner_force, 1, 1),
    )
    return (disp_new, veloc_new, mu_new, kappa_new)


def solution(mesh):
    return jax.shard_map(
        local,
        mesh=mesh,
        in_specs=(
            P(None, "gx", "gy", None),
            P(None, "gx", "gy", None),
            P(None, "gx", "gy", None),
            P("gx", "gy", None),
            P("gx", "gy", None),
            P("gx", "gy", None),
            P(None, ("gx", "gy")),
            P(None, ("gx", "gy")),
            P(None, ("gx", "gy")),
            P(None, ("gx", "gy")),
            P(None, ("gx", "gy")),
            P(("gx", "gy"), None),
            P(("gx", "gy")),
        ),
        out_specs=(
            P(None, "gx", "gy", None),
            P(None, "gx", "gy", None),
            P(None, ("gx", "gy")),
            P(None, ("gx", "gy")),
        ),
        check_vma=False,
    )
```
